256 devices in a mesh: gx: 16 (over x, y_lo, core), ha: 16 (over z, y_hi).
Axes of the slice: x: 4, y: 4 (y_hi: 2, y_lo: 2; y = y_hi * 2 + y_lo), z: 8, core: 2. Of those that a mesh axis runs over, the one named last changes fastest.
Arguments:
- value_field: float32 [4, 64, 128, 128], P(None, 'gx', 'ha'), may hold values from -6 to 6
- wind_grid: int32 [2, 2, 64, 128], P(None, None, 'gx'), may hold values from -1023 to 1023
- obstacle: int32 [64, 128], P('gx'), may hold values 0 or 1
Outputs:
- value_next: float32 [4, 64, 128, 128], P(None, 'gx', 'ha')
The draws below stay inside these ranges and needn't reach their ends.
All inputs are finite; a program needn't handle non-finite values. Where the reference program divides by a largest or mean magnitude, that divisor is 1e-20 or more. No bound on the sum of `obstacle` on one device may be relied on, other than what follows from the above.
Results may differ from the reference program's by a relative error of at most 0.0003.
Values sent between devices are 32-bit elements; how exact they have to be, the bound alone decides.
A program may use at most 64 MiB of HBM per device.

```python
import math
import jax
import jax.numpy as jnp
from jax import lax

NS = 4
NH = 128
CX = 4
NY = 128
STEPS = 2
NX = 64
N_GX = 16


def draw_wind_grid(key, part):
    key = jax.random.fold_in(key, 11)
    peak_key, pick_key, base_key, row_key, column_key, spread_key = jax.random.split(key, 6)
    pair_count = STEPS * 2
    peak_values = jax.random.randint(peak_key, (pair_count,), 256, 1024, dtype=jnp.int32)
    chosen = jax.random.randint(pick_key, (), 0, pair_count, dtype=jnp.int32)
    peak_values = jnp.where(jnp.arange(pair_count, dtype=jnp.int32) == chosen, 1023, peak_values)
    peak_values = peak_values.reshape(STEPS, 2, 1, 1)
    spread_values = jax.random.randint(spread_key, (STEPS, 2, 1, 1), 256, 1024, dtype=jnp.int32)
    x_index = jnp.arange(NX, dtype=jnp.int32)[None, None, :, None]
    y_index = jnp.arange(NY, dtype=jnp.int32)[None, None, None, :]
    bound = spread_values * (NX - 1 + 2 * x_index) // (6 * (NX - 1))
    drawn = jax.random.randint(base_key, (STEPS, 2, NX, NY), -bound, bound + 1, dtype=jnp.int32)
    peak_row = jax.random.randint(row_key, (STEPS, 2, 1, 1), 0, NX, dtype=jnp.int32)
    peak_column = jax.random.randint(column_key, (STEPS, 2, 1, 1), 0, NY, dtype=jnp.int32)
    on_row = x_index == peak_row
    drawn = jnp.where(on_row & (y_index == peak_column), peak_values, drawn)
    drawn = jnp.where(on_row & (y_index == (peak_column + 1) % NY), -peak_values, drawn)
    return drawn


def touch_ends(values, own_key, low, largest):
    longest = values.shape.index(max(values.shape))
    spots = []
    for shift in (0, 1):
        where = [jax.random.randint(jax.random.fold_in(own_key, axis), (), 0, length) for axis, length in enumerate(values.shape)]
        where[longest] = (where[longest] + shift) % values.shape[longest]
        spots.append(tuple(where))
    return values.at[spots[0]].set(low).at[spots[1]].set(largest)


def levels(key, dims, shards, low, high):
    factor_of, own = 1.0, jax.random.fold_in(key, 6)
    for dim, shards_of in shards:
        draws = jnp.exp(jax.random.uniform(jax.random.fold_in(own, dim), (shards_of,), jnp.float32, low / len(shards), high / len(shards)))
        factor_of = factor_of * jnp.repeat(draws, dims[dim] // shards_of).reshape([-1 if axis == dim else 1 for axis in range(len(dims))])
    return factor_of


def noise(own_key, shape, deviation, limit, shards=(), kind=jnp.bfloat16):
    values = jax.random.normal(own_key, shape, jnp.float32) * deviation
    if len(shards) > 0:
        values = levels(own_key, shape, shards, -0.22, 0.18) * values
    return jnp.clip(values, min=-limit, max=limit).astype(kind)


def setup_inputs(seed: int = 0) -> dict:
    arg_keys = jax.random.split(jax.random.key(seed), 4)
    value_field = noise(arg_keys[0], (NS, NX, NH, NY), 1.0, 6.0, ((1, 16), (2, 16)), jnp.float32)
    wind_grid = draw_wind_grid(jax.random.fold_in(arg_keys[3], 71), 0)
    obstacle = touch_ends((jax.random.randint(arg_keys[2], (NX, NY), 0, 6) < 1).astype(jnp.int32), jax.random.fold_in(arg_keys[2], 1), 0, 1)
    return {"value_field": value_field, "wind_grid": wind_grid, "obstacle": obstacle}


TURN_RATE = 0.25
ACCEL_MAX = 0.5
SPEED_BASE = 0.5
SPEED_STEP = 0.25
SPEED_MAX = 1.25
WIND_SCALE = 1.0 / 512.0
CFL_NUMBER = 0.8
OBSTACLE_LEVEL = 1.0


def minmod(left_term, right_term):
    return 0.5 * (jnp.sign(left_term) + jnp.sign(right_term)) * jnp.minimum(jnp.abs(left_term), jnp.abs(right_term))


def part_of(source, begin, finish, dimension):
    return lax.slice_in_dim(source, begin, finish, axis=dimension)


def slopes(padded, dimension, spacing):
    padded_extent = padded.shape[dimension]
    inner_count = padded_extent - 4
    first_diff = part_of(padded, 1, padded_extent, dimension) - part_of(padded, 0, padded_extent - 1, dimension)
    second_diff = part_of(first_diff, 1, inner_count + 3, dimension) - part_of(first_diff, 0, inner_count + 2, dimension)
    limited = minmod(part_of(second_diff, 0, inner_count + 1, dimension), part_of(second_diff, 1, inner_count + 2, dimension))
    backward = (part_of(first_diff, 1, inner_count + 1, dimension) + 0.5 * part_of(limited, 0, inner_count, dimension)) / spacing
    forward = (part_of(first_diff, 2, inner_count + 2, dimension) - 0.5 * part_of(limited, 1, inner_count + 1, dimension)) / spacing
    return 0.5 * (backward + forward), forward - backward


def extend(source, dimension):
    extent = source.shape[dimension]
    first_plane = part_of(source, 0, 1, dimension)
    second_plane = part_of(source, 1, 2, dimension)
    last_plane = part_of(source, extent - 1, extent, dimension)
    before_plane = part_of(source, extent - 2, extent - 1, dimension)
    return jnp.concatenate([3.0 * first_plane - 2.0 * second_plane, 2.0 * first_plane - second_plane, source,
                            2.0 * last_plane - before_plane, 3.0 * last_plane - 2.0 * before_plane], axis=dimension)


def rate(center, along_x, along_head, wind_x, wind_y, head_cos, head_sin, alpha_x, alpha_y, head_step):
    mean_x, jump_x = slopes(along_x, 1, 1.0)
    mean_h, jump_h = slopes(along_head, 2, head_step)
    mean_y, jump_y = slopes(extend(center, 3), 3, 1.0)
    mean_s, jump_s = slopes(extend(center, 0), 0, SPEED_STEP)
    speeds = (SPEED_BASE + SPEED_STEP * jnp.arange(center.shape[0], dtype=jnp.float32))[:, None, None, None]
    velocity_x = speeds * head_cos[None, None, :, None] + wind_x[None, :, None, :]
    velocity_y = speeds * head_sin[None, None, :, None] + wind_y[None, :, None, :]
    hamilton = mean_x * velocity_x + mean_y * velocity_y - TURN_RATE * jnp.abs(mean_h) - ACCEL_MAX * jnp.abs(mean_s)
    return hamilton + 0.5 * (alpha_x * jump_x + alpha_y * jump_y + TURN_RATE * jump_h + ACCEL_MAX * jump_s)


def time_step(alpha_x, alpha_y, head_step):
    return CFL_NUMBER / (alpha_x + alpha_y + TURN_RATE / head_step + ACCEL_MAX / SPEED_STEP)


def full_rate(field, wind_x, wind_y, alpha_x, alpha_y, head_step):
    along_x = extend(field, 1)
    along_head = jnp.concatenate([field[:, :, -2:], field, field[:, :, :2]], axis=2)
    angles = jnp.arange(NH, dtype=jnp.float32) * head_step
    head_cos = jnp.cos(angles)
    head_sin = jnp.sin(angles)

    def block_rate(block_index):
        offset = (block_index * CX).astype(jnp.int32)
        center = lax.dynamic_slice_in_dim(field, offset, CX, 1)
        wide_rows = lax.dynamic_slice_in_dim(along_x, offset, CX + 4, 1)
        cycle_rows = lax.dynamic_slice_in_dim(along_head, offset, CX, 1)
        wind_part_x = lax.dynamic_slice_in_dim(wind_x, offset, CX, 0)
        wind_part_y = lax.dynamic_slice_in_dim(wind_y, offset, CX, 0)
        return rate(center, wide_rows, cycle_rows, wind_part_x, wind_part_y, head_cos, head_sin, alpha_x, alpha_y, head_step)

    blocks = lax.map(block_rate, jnp.arange(N_GX, dtype=jnp.int32))
    return jnp.transpose(blocks, (1, 0, 2, 3, 4)).reshape(field.shape)


def reference(value_field, wind_grid, obstacle):
    head_step = 2.0 * math.pi / NH
    blocked = (obstacle == 1)[None, :, None, :]
    field = value_field
    for step_index in range(STEPS):
        wind_x = wind_grid[step_index, 0].astype(jnp.float32) * WIND_SCALE
        wind_y = wind_grid[step_index, 1].astype(jnp.float32) * WIND_SCALE
        alpha_x = SPEED_MAX + jnp.max(jnp.abs(wind_x))
        alpha_y = SPEED_MAX + jnp.max(jnp.abs(wind_y))
        delta_time = time_step(alpha_x, alpha_y, head_step)
        section = field + delta_time * full_rate(field, wind_x, wind_y, alpha_x, alpha_y, head_step)
        candidate = 0.5 * field + 0.5 * (section + delta_time * full_rate(section, wind_x, wind_y, alpha_x, alpha_y, head_step))
        field = jnp.where(blocked, jnp.maximum(candidate, OBSTACLE_LEVEL), candidate)
    return field
```

```python
import functools
import math

import jax
import jax.numpy as jnp
from jax import lax
from jax.experimental import pallas as pl
from jax.experimental.pallas import tpu as pltpu
from jax.sharding import PartitionSpec as P

MESH = pl.DeviceIdType.MESH
STEPS = 2
TURN_RATE = 0.25
ACCEL_MAX = 0.5
SPEED_BASE = 0.5
SPEED_STEP = 0.25
SPEED_MAX = 1.25
WIND_SCALE = 1.0 / 512.0
CFL_NUMBER = 0.8
OBSTACLE_LEVEL = 1.0
F32 = jnp.float32

LEFT, RIGHT, UP, DOWN = 0, 1, 2, 3
CORNERS = ((1, 1), (1, -1), (-1, 1), (-1, -1))


def limiter(before, here):
    return jnp.maximum(jnp.minimum(before, jnp.maximum(here, 0.0)), jnp.minimum(here, 0.0))


def face_parts(values):
    n = values.shape[0] - 4
    diff = values[1:] - values[:-1]
    half = 0.5 * diff
    curve = half[1:] - half[:-1]
    limited = limiter(curve[:-1], curve[1:])
    inner = diff[1 : n + 2]
    return inner[:n] + limited[:n], inner[1:] - limited[1:]


def lane_parts(values):
    lanes = lax.broadcasted_iota(jnp.int32, values.shape, values.ndim - 1)
    axis, extent = values.ndim - 1, values.shape[-1]
    diff = values - pltpu.roll(values, 1, axis)
    after = pltpu.roll(diff, extent - 1, axis)
    diff = jnp.where(lanes == 0, after, diff)
    after = jnp.where(lanes == extent - 1, diff, after)
    curve = 0.5 * (after - diff)
    limited = limiter(pltpu.roll(curve, 1, axis), curve)
    return diff + limited, after - pltpu.roll(limited, extent - 1, axis)


def heading_term(here, other):
    rows = lax.broadcasted_iota(jnp.int32, here.shape, here.ndim - 2)
    axis = here.ndim - 2
    low2 = pltpu.roll(jnp.where(rows >= 6, other, here), 2, axis)
    low1 = pltpu.roll(jnp.where(rows == 7, other, here), 1, axis)
    up1 = pltpu.roll(jnp.where(rows == 0, other, here), 7, axis)
    up2 = pltpu.roll(jnp.where(rows <= 1, other, here), 6, axis)
    diff0, diff1, diff2, diff3 = low1 - low2, here - low1, up1 - here, up2 - up1
    curve0, curve1, curve2 = 0.5 * (diff1 - diff0), 0.5 * (diff2 - diff1), 0.5 * (diff3 - diff2)
    return jnp.maximum(limiter(curve0, curve1) + diff1, limiter(curve1, curve2) - diff2)


def speed_term(s, values):
    if s == 0:
        return jnp.abs(values[1] - values[0])
    if s == 3:
        return jnp.abs(values[3] - values[2])
    diff1, diff2, diff3 = values[1] - values[0], values[2] - values[1], values[3] - values[2]
    limited = limiter(0.5 * (diff2 - diff1), 0.5 * (diff3 - diff2))
    if s == 1:
        return jnp.maximum(diff1, limited - diff2)
    return jnp.maximum(diff2 + limited, -diff3)


def kernel(
    n_gx, n_ha, field_hbm, wind_hbm, obstacle_hbm, out_hbm,
    v_a, w_a, v_b, w_b, sec_t, sec_w, wind_int, wind_f, obst, peaks, trig, out_v,
    send_sem, recv_sem, wind_send, wind_recv, local_sem,
):
    gx, ha = lax.axis_index("gx"), lax.axis_index("ha")
    head_step = 2.0 * math.pi / (8 * n_ha)

    loads = [
        pltpu.make_async_copy(wind_hbm, wind_int.at[:, :, 2:6], local_sem.at[0]),
        pltpu.make_async_copy(field_hbm, v_a.at[:, 4:8], local_sem.at[1]),
        pltpu.make_async_copy(obstacle_hbm, obst, local_sem.at[2]),
    ]
    for copy in loads:
        copy.start()

    def has(dx):
        return (gx + dx >= 0) & (gx + dx < n_gx)

    barrier = pltpu.get_barrier_semaphore()
    for k in range(1, n_gx):
        pl.semaphore_signal(barrier, inc=1, device_id=(lax.rem(gx + k, n_gx), ha), device_id_type=MESH)
    for dh in (1, n_ha - 1):
        pl.semaphore_signal(barrier, inc=1, device_id=(gx, lax.rem(ha + dh, n_ha)), device_id_type=MESH)
    for dx in (1, -1):
        @pl.when(has(dx))
        def _():
            for dh in (1, n_ha - 1):
                pl.semaphore_signal(
                    barrier, inc=1, device_id=(gx + dx, lax.rem(ha + dh, n_ha)), device_id_type=MESH
                )

    loads[0].wait()
    for step in range(STEPS):
        for part in range(2):
            own = jnp.abs(wind_int[step, part, 2:6, :].astype(F32) * WIND_SCALE)
            peaks[n_gx - 1, pl.ds(2 * step + part, 1), :] = jnp.max(own, axis=0, keepdims=True)
    rows = lax.broadcasted_iota(jnp.int32, (8, 128), 0)
    total = 8 * n_ha
    for tile in range(2):
        place = rows if tile == 0 else jnp.where(rows < 4, rows + 8, rows - 8)
        place = lax.rem(ha * 8 + place + total, total)
        angle = place.astype(F32) * head_step
        trig[tile, 0] = jnp.cos(angle)
        trig[tile, 1] = jnp.sin(angle)
    loads[1].wait()

    pl.semaphore_wait(
        barrier, n_gx + 1 + 2 * (has(1).astype(jnp.int32) + has(-1).astype(jnp.int32))
    )

    def remote(src, dst, index, dx, dh):
        return pltpu.make_async_remote_copy(
            src_ref=src, dst_ref=dst, send_sem=send_sem.at[index], recv_sem=recv_sem.at[index],
            device_id=(gx + dx, lax.rem(ha + dh + n_ha, n_ha)), device_id_type=MESH,
        )

    def halo(v, w, base):
        copies = [
            (0, remote(v.at[:, 4:8, 4:8], w.at[:, 2:6, 4:8], base, 0, 1)),
            (0, remote(v.at[:, 4:8, 0:4], w.at[:, 2:6, 0:4], base + 1, 0, -1)),
        ]
        for n, (dx, dh) in enumerate(CORNERS):
            band = slice(6, 8) if dh > 0 else slice(0, 2)
            near, far = (slice(6, 8), slice(0, 2)) if dx > 0 else (slice(4, 6), slice(6, 8))
            copies.append((dx, remote(v.at[:, near, band], w.at[:, far, band], base + 2 + n, dx, dh)))
        copies.append((1, remote(v.at[:, 4:8], v.at[:, 0:4], base + 6, 1, 0)))
        copies.append((-1, remote(v.at[:, 4:8], v.at[:, 8:12], base + 7, -1, 0)))
        return copies

    def at(dx, action):
        if dx == 0:
            action()
        else:
            pl.when(has(dx))(action)

    first = halo(v_a, w_a, 0)
    second = halo(v_b, w_b, 8)
    wind_edges = [
        (1, remote(wind_int.at[:, :, 4:6], wind_int.at[:, :, 0:2], 16, 1, 0)),
        (-1, remote(wind_int.at[:, :, 2:4], wind_int.at[:, :, 6:8], 17, -1, 0)),
    ]
    wind_copies = [
        pltpu.make_async_remote_copy(
            src_ref=peaks.at[n_gx - 1], dst_ref=peaks.at[k - 1],
            send_sem=wind_send.at[k - 1], recv_sem=wind_recv.at[k - 1],
            device_id=(lax.rem(gx + k, n_gx), ha), device_id_type=MESH,
        )
        for k in range(1, n_gx)
    ]
    for dx, copy in first[:2]:
        at(dx, copy.start)
    for copy in wind_copies:
        copy.start()
    for dx, copy in first[2:] + wind_edges:
        at(dx, copy.start)

    for dx, copy in wind_edges:
        at(-dx, copy.wait_recv)
    for step in range(STEPS):
        for part in range(2):
            for plane in range(8):
                row = wind_int[step, part, pl.ds(plane, 1), :].astype(F32) * WIND_SCALE
                wind_f[step, part, plane] = jnp.broadcast_to(row, (8, 128))
    for copy in wind_copies:
        copy.wait_recv()
    highest = jnp.max(peaks[...], axis=0)
    highest = jnp.max(highest, axis=1, keepdims=True)
    alphas, halves = [], []
    for step in range(STEPS):
        pair = [
            jnp.broadcast_to(SPEED_MAX + highest[2 * step + part : 2 * step + part + 1], (8, 128))
            for part in range(2)
        ]
        alphas.append(pair)
        halves.append(
            (0.5 * CFL_NUMBER)
            / (pair[0] + pair[1] + (TURN_RATE / head_step + ACCEL_MAX / SPEED_STEP))
        )

    def gain(step, s, tile, first_plane, around_x, here, other, speeds_here):
        speed = SPEED_BASE + SPEED_STEP * s
        alpha_x, alpha_y = alphas[step]
        back, fore = face_parts(around_x)
        velocity = speed * trig[tile, 0] + wind_f[step, 0, first_plane : first_plane + 4]
        result = (back + fore) * velocity + alpha_x * (fore - back)
        back, fore = lane_parts(here)
        velocity = speed * trig[tile, 1] + wind_f[step, 1, first_plane : first_plane + 4]
        result = result + (back + fore) * velocity + alpha_y * (fore - back)
        result = result - (2.0 * TURN_RATE / head_step) * heading_term(here, other)
        return result - (2.0 * ACCEL_MAX / SPEED_STEP) * speed_term(s, speeds_here)

    def advance(step, v, w, finish):
        half = halves[step]

        def ends(ref, low, count):
            @pl.when(gx == 0)
            def _():
                a, b = ref[:, low], ref[:, low + 1]
                ref[:, low - 1] = 2.0 * a - b
                ref[:, low - 2] = 3.0 * a - 2.0 * b

            @pl.when(gx == n_gx - 1)
            def _():
                a, b = ref[:, low + count - 1], ref[:, low + count - 2]
                ref[:, low + count] = 2.0 * a - b
                ref[:, low + count + 1] = 3.0 * a - 2.0 * b

        ends(v, 4, 4)
        ends(w, 2, 4)
        for s in range(4):
            for block in (0, 4):
                here = v[s, block + 2 : block + 6]
                speeds = [v[i, block + 2 : block + 6] for i in range(4)]
                sec_t[s, block : block + 4] = here + half * gain(
                    step, s, 0, block, v[s, block : block + 8], here, w[s, block : block + 4], speeds
                )
            here = w[s, 2:6]
            speeds = [w[i, 2:6] for i in range(4)]
            sec_w[s] = here + half * gain(step, s, 1, 2, w[s], here, v[s, 4:8], speeds)
        ends(sec_t, 2, 4)
        for s in range(4):
            here = sec_t[s, 2:6]
            speeds = [sec_t[i, 2:6] for i in range(4)]
            change = half * gain(step, s, 0, 2, sec_t[s], here, sec_w[s], speeds)
            finish(s, 0.5 * (v[s, 4:8] + (here + change)))

    def limit(s, candidate, plane):
        blocked = jnp.broadcast_to(obst[pl.ds(plane, 1), :], (8, 128)) == 1
        value = candidate[plane]
        return jnp.where(blocked, jnp.maximum(value, OBSTACLE_LEVEL), value)

    def keep(s, candidate):
        for plane in range(4):
            v_b[s, 4 + plane] = limit(s, candidate, plane)

    def give(s, candidate):
        for plane in range(4):
            out_v[s, plane] = limit(s, candidate, plane)

    for dx, copy in first:
        at(-dx, copy.wait_recv)
    loads[2].wait()
    advance(0, v_a, w_a, keep)
    for dx, copy in second:
        at(dx, copy.start)
    for dx, copy in first + wind_edges:
        at(dx, copy.wait_send)
    for copy in wind_copies:
        copy.wait_send()
    for dx, copy in second:
        at(-dx, copy.wait_recv)
    advance(1, v_b, w_b, give)
    result = pltpu.make_async_copy(out_v, out_hbm, local_sem.at[3])
    result.start()
    for dx, copy in second:
        at(dx, copy.wait_send)
    result.wait()


def solution(mesh):
    n_gx, n_ha = mesh.shape["gx"], mesh.shape["ha"]

    def local(value_field, wind_grid, obstacle):
        return pl.pallas_call(
            functools.partial(kernel, n_gx, n_ha),
            out_shape=jax.ShapeDtypeStruct(value_field.shape, F32),
            in_specs=[pl.BlockSpec(memory_space=pl.ANY)] * 3,
            out_specs=pl.BlockSpec(memory_space=pl.ANY),
            scratch_shapes=[
                pltpu.VMEM((4, 12, 8, 128), F32),
                pltpu.VMEM((4, 8, 8, 128), F32),
                pltpu.VMEM((4, 12, 8, 128), F32),
                pltpu.VMEM((4, 8, 8, 128), F32),
                pltpu.VMEM((4, 8, 8, 128), F32),
                pltpu.VMEM((4, 4, 8, 128), F32),
                pltpu.VMEM((2, 2, 8, 128), jnp.int32),
                pltpu.VMEM((2, 2, 8, 8, 128), F32),
                pltpu.VMEM((4, 128), jnp.int32),
                pltpu.VMEM((n_gx, 4, 128), F32),
                pltpu.VMEM((2, 2, 8, 128), F32),
                pltpu.VMEM((4, 4, 8, 128), F32),
                pltpu.SemaphoreType.DMA((18,)),
                pltpu.SemaphoreType.DMA((18,)),
                pltpu.SemaphoreType.DMA((n_gx - 1,)),
                pltpu.SemaphoreType.DMA((n_gx - 1,)),
                pltpu.SemaphoreType.DMA((4,)),
            ],
            compiler_params=pltpu.CompilerParams(collective_id=0, has_side_effects=True),
            name="reach",
        )(value_field, wind_grid, obstacle)

    placed = (P(None, "gx", "ha", None), P(None, None, "gx", None), P("gx", None))
    return jax.shard_map(
        local, mesh=mesh, in_specs=placed, out_specs=P(None, "gx", "ha", None), check_vma=False
    )
```

```python
import functools
import math

import jax
import jax.numpy as jnp
from jax import lax
from jax.experimental import pallas as pl
from jax.experimental.pallas import tpu as pltpu
from jax.sharding import PartitionSpec as P

MESH = pl.DeviceIdType.MESH
STEPS = 2
TURN_RATE = 0.25
ACCEL_MAX = 0.5
SPEED_BASE = 0.5
SPEED_STEP = 0.25
SPEED_MAX = 1.25
WIND_SCALE = 1.0 / 512.0
CFL_NUMBER = 0.8
OBSTACLE_LEVEL = 1.0
F32 = jnp.float32

CORNERS = ((1, 1), (1, -1), (-1, 1), (-1, -1))


def limiter(before, here):
    return jnp.maximum(jnp.minimum(before, jnp.maximum(here, 0.0)), jnp.minimum(here, 0.0))


def parts(diff0, diff1, diff2, diff3):
    curve = diff2 - diff1
    backward = diff1 + 0.5 * limiter(diff1 - diff0, curve)
    forward = diff2 - 0.5 * limiter(curve, diff3 - diff2)
    return backward, forward


def plane_parts(values):
    n = values.shape[1] - 4
    diff = values[:, 1:] - values[:, :-1]
    curve = diff[:, 1:] - diff[:, :-1]
    limited = 0.5 * limiter(curve[:, :-1], curve[:, 1:])
    inner = diff[:, 1 : n + 2]
    return inner[:, :n] + limited[:, :n], inner[:, 1:] - limited[:, 1:]


def lane_parts(here):
    axis, extent = here.ndim - 1, here.shape[-1]
    lanes = lax.broadcasted_iota(jnp.int32, here.shape, axis)
    low1, low2 = pltpu.roll(here, 1, axis), pltpu.roll(here, 2, axis)
    up1, up2 = pltpu.roll(here, extent - 1, axis), pltpu.roll(here, extent - 2, axis)
    below, above = here - low1, up1 - here
    diff1 = jnp.where(lanes == 0, above, below)
    diff2 = jnp.where(lanes == extent - 1, below, above)
    diff0 = jnp.where(lanes <= 1, diff1, low1 - low2)
    diff3 = jnp.where(lanes >= extent - 2, diff2, up2 - up1)
    return parts(diff0, diff1, diff2, diff3)


def heading_term(here, other):
    axis = here.ndim - 2
    rows = lax.broadcasted_iota(jnp.int32, here.shape, axis)
    low2 = pltpu.roll(jnp.where(rows >= 6, other, here), 2, axis)
    low1 = pltpu.roll(jnp.where(rows == 7, other, here), 1, axis)
    up1 = pltpu.roll(jnp.where(rows == 0, other, here), 7, axis)
    up2 = pltpu.roll(jnp.where(rows <= 1, other, here), 6, axis)
    backward, forward = parts(low1 - low2, here - low1, up1 - here, up2 - up1)
    return jnp.maximum(backward, -forward)


def speed_terms(values):
    diff = [values[i + 1] - values[i] for i in range(3)]
    limited = 0.5 * limiter(diff[1] - diff[0], diff[2] - diff[1])
    return jnp.stack([
        jnp.abs(diff[0]),
        jnp.maximum(diff[0], limited - diff[1]),
        jnp.maximum(diff[1] + limited, -diff[2]),
        jnp.abs(diff[2]),
    ])


def kernel(
    n_gx, n_ha, field_hbm, wind_hbm, obstacle_hbm, out_v,
    v_a, w_a, v_b, w_b, sec_t, sec_w, known, jump_x, jump_y, wind_int, wind_f, obst, peaks, drift,
    send_sem, recv_sem, wind_send, wind_recv, local_sem,
):
    gx, ha = lax.axis_index("gx"), lax.axis_index("ha")
    head_step = 2.0 * math.pi / (8 * n_ha)

    loads = [
        pltpu.make_async_copy(wind_hbm, wind_int.at[:, :, 2:6], local_sem.at[0]),
        pltpu.make_async_copy(field_hbm, v_a.at[:, 4:8], local_sem.at[1]),
        pltpu.make_async_copy(obstacle_hbm, obst, local_sem.at[2]),
    ]
    for copy in loads:
        copy.start()

    def has(dx):
        return (gx + dx >= 0) & (gx + dx < n_gx)

    barrier = pltpu.get_barrier_semaphore()
    for k in range(1, n_gx):
        pl.semaphore_signal(barrier, inc=1, device_id=(lax.rem(gx + k, n_gx), ha), device_id_type=MESH)
    for dh in (1, n_ha - 1):
        pl.semaphore_signal(barrier, inc=1, device_id=(gx, lax.rem(ha + dh, n_ha)), device_id_type=MESH)
    for dx in (1, -1):
        @pl.when(has(dx))
        def _():
            for dh in (1, n_ha - 1):
                pl.semaphore_signal(
                    barrier, inc=1, device_id=(gx + dx, lax.rem(ha + dh, n_ha)), device_id_type=MESH
                )

    loads[0].wait()
    for step in range(STEPS):
        for part in range(2):
            own = jnp.abs(wind_int[step, part, 2:6, :].astype(F32) * WIND_SCALE)
            peaks[n_gx - 1, pl.ds(2 * step + part, 1), :] = jnp.max(own, axis=0, keepdims=True)
    rows = lax.broadcasted_iota(jnp.int32, (8, 128), 0)
    total = 8 * n_ha
    for tile in range(2):
        place = rows if tile == 0 else jnp.where(rows < 4, rows + 8, rows - 8)
        place = lax.rem(ha * 8 + place + total, total)
        angle = place.astype(F32) * head_step
        for part, value in enumerate((jnp.cos(angle), jnp.sin(angle))):
            for s in range(4):
                drift[tile, part, s] = (SPEED_BASE + SPEED_STEP * s) * value
    loads[1].wait()

    pl.semaphore_wait(
        barrier, n_gx + 1 + 2 * (has(1).astype(jnp.int32) + has(-1).astype(jnp.int32))
    )

    def remote(src, dst, index, dx, dh):
        return pltpu.make_async_remote_copy(
            src_ref=src, dst_ref=dst, send_sem=send_sem.at[index], recv_sem=recv_sem.at[index],
            device_id=(gx + dx, lax.rem(ha + dh + n_ha, n_ha)), device_id_type=MESH,
        )

    def halo(v, w, base, part):
        copies = [
            (0, remote(v.at[part, 4:8, 4:8], w.at[part, 2:6, 4:8], base, 0, 1)),
            (0, remote(v.at[part, 4:8, 0:4], w.at[part, 2:6, 0:4], base + 1, 0, -1)),
        ]
        for n, (dx, dh) in enumerate(CORNERS):
            band = slice(6, 8) if dh > 0 else slice(0, 2)
            near, far = (slice(6, 8), slice(0, 2)) if dx > 0 else (slice(4, 6), slice(6, 8))
            copies.append((dx, remote(v.at[part, near, band], w.at[part, far, band], base + 2 + n, dx, dh)))
        copies.append((1, remote(v.at[part, 4:8], v.at[part, 0:4], base + 6, 1, 0)))
        copies.append((-1, remote(v.at[part, 4:8], v.at[part, 8:12], base + 7, -1, 0)))
        return copies

    def start(copies):
        for dx in (0, 1, -1):
            mine = [copy for d, copy in copies if d == dx]

            def run(mine=mine):
                for copy in mine:
                    copy.start()

            guarded(dx, mine, run)

    def receive(copies):
        for dx in (0, 1, -1):
            mine = [copy for d, copy in copies if d == dx]

            def run(mine=mine):
                for copy in mine:
                    copy.wait_recv()

            guarded(-dx, mine, run)

    def finish_sends(copies):
        for dx in (0, 1, -1):
            mine = [copy for d, copy in copies if d == dx]

            def run(mine=mine):
                for copy in mine:
                    copy.wait_send()

            guarded(dx, mine, run)

    def guarded(dx, mine, run):
        if not mine:
            return
        if dx == 0:
            run()
        else:
            pl.when(has(dx))(run)

    first = halo(v_a, w_a, 0, slice(0, 4))
    second = halo(v_b, w_b, 10, slice(0, 4))
    wind_edges = [
        (1, remote(wind_int.at[:, :, 4:6], wind_int.at[:, :, 0:2], 8, 1, 0)),
        (-1, remote(wind_int.at[:, :, 2:4], wind_int.at[:, :, 6:8], 9, -1, 0)),
    ]
    wind_copies = [
        pltpu.make_async_remote_copy(
            src_ref=peaks.at[n_gx - 1], dst_ref=peaks.at[k - 1],
            send_sem=wind_send.at[k - 1], recv_sem=wind_recv.at[k - 1],
            device_id=(lax.rem(gx + k, n_gx), ha), device_id_type=MESH,
        )
        for k in range(1, n_gx)
    ]
    start(first[:2])
    for copy in wind_copies:
        copy.start()
    start(first[2:] + wind_edges)

    half_scale = ACCEL_MAX / SPEED_STEP * 2.0
    head_scale = 2.0 * TURN_RATE / head_step
    own, left, right = slice(4, 8), slice(2, 4), slice(8, 10)

    def ends(ref, low, count):
        for at_end, edge, next_one, near, far in (
            (gx == 0, low, low + 1, low - 1, low - 2),
            (gx == n_gx - 1, low + count - 1, low + count - 2, low + count, low + count + 1),
        ):
            a, b = ref[:, edge], ref[:, next_one]
            ref[:, near] = jnp.where(at_end, 2.0 * a - b, ref[:, near])
            ref[:, far] = jnp.where(at_end, 3.0 * a - 2.0 * b, ref[:, far])

    def across(step, tile, planes, here):
        back, fore = lane_parts(here)
        velocity = drift[tile, 1][:, None] + wind_f[step, 1, planes][None]
        return (back + fore) * velocity, fore - back

    def along(step, tile, planes, around):
        back, fore = plane_parts(around)
        velocity = drift[tile, 0][:, None] + wind_f[step, 0, planes][None]
        return (back + fore) * velocity, fore - back

    def begin(step, v, planes):
        place = slice(planes.start - 2, planes.stop - 2)
        values = v[:, planes]
        mean, jump = across(step, 0, place, values)
        known[:, place] = mean - half_scale * speed_terms(values)
        jump_y[:, place] = jump

    def extend_x(step, v):
        for block in (0, 4):
            place = slice(block, block + 4)
            mean, jump = along(step, 0, place, v[:, block : block + 8])
            known[:, place] = known[:, place] + mean
            jump_x[:, place] = jump

    def whole(step, tile, planes, around, here, other):
        alpha_x, alpha_y = alphas[step]
        mean_x, jump_at_x = along(step, tile, planes, around)
        mean_y, jump_at_y = across(step, tile, planes, here)
        result = mean_x + mean_y + alpha_x * jump_at_x + alpha_y * jump_at_y
        return halves[step] * (
            result - head_scale * heading_term(here, other) - half_scale * speed_terms(here)
        )

    def first_stage(step, v, w):
        alpha_x, alpha_y = alphas[step]
        for block in (0, 4):
            place = slice(block, block + 4)
            here, other = v[:, block + 2 : block + 6], w[:, place]
            rest = known[:, place] + alpha_x * jump_x[:, place] + alpha_y * jump_y[:, place]
            sec_t[:, place] = here + halves[step] * (rest - head_scale * heading_term(here, other))
        here = w[:, 2:6]
        sec_w[...] = here + whole(step, 1, slice(2, 6), w[...], here, v[:, own])

    def second_stage(step, v, finish):
        ends(sec_t, 2, 4)
        here = sec_t[:, 2:6]
        change = whole(step, 0, slice(2, 6), sec_t[...], here, sec_w[...])
        finish(0.5 * (v[:, own] + (here + change)))

    def limit(candidate, plane):
        blocked = jnp.broadcast_to(obst[pl.ds(plane, 1), :], (8, 128)) == 1
        value = candidate[:, plane]
        return jnp.where(blocked[None], jnp.maximum(value, OBSTACLE_LEVEL), value)

    def keep(candidate):
        for plane in range(4):
            v_b[:, 4 + plane] = limit(candidate, plane)
        start(second)

    def give(candidate):
        for plane in range(4):
            out_v[:, plane] = limit(candidate, plane)

    def spread(planes):
        for step in range(STEPS):
            for part in range(2):
                for plane in planes:
                    row = wind_int[step, part, pl.ds(plane, 1), :].astype(F32) * WIND_SCALE
                    wind_f[step, part, plane] = jnp.broadcast_to(row, (8, 128))

    spread(range(2, 6))
    begin(0, v_a, own)
    receive(wind_edges + first[6:])
    spread((0, 1, 6, 7))
    ends(v_a, 4, 4)
    begin(0, v_a, left)
    begin(0, v_a, right)
    extend_x(0, v_a)

    for copy in wind_copies:
        copy.wait_recv()
    highest = jnp.max(peaks[...], axis=0)
    highest = jnp.max(highest, axis=1, keepdims=True)
    alphas, halves = [], []
    for step in range(STEPS):
        pair = [
            jnp.broadcast_to(SPEED_MAX + highest[2 * step + part : 2 * step + part + 1], (8, 128))
            for part in range(2)
        ]
        alphas.append(pair)
        halves.append(
            (0.5 * CFL_NUMBER)
            / (pair[0] + pair[1] + (TURN_RATE / head_step + ACCEL_MAX / SPEED_STEP))
        )

    receive(first[:6])
    loads[2].wait()
    ends(w_a, 2, 4)
    first_stage(0, v_a, w_a)
    second_stage(0, v_a, keep)

    begin(1, v_b, own)
    receive(second[6:])
    ends(v_b, 4, 4)
    begin(1, v_b, left)
    begin(1, v_b, right)
    extend_x(1, v_b)
    receive(second[:6])
    ends(w_b, 2, 4)
    first_stage(1, v_b, w_b)
    second_stage(1, v_b, give)
    finish_sends(first + wind_edges + second)
    for copy in wind_copies:
        copy.wait_send()


def solution(mesh):
    n_gx, n_ha = mesh.shape["gx"], mesh.shape["ha"]

    def local(value_field, wind_grid, obstacle):
        return pl.pallas_call(
            functools.partial(kernel, n_gx, n_ha),
            out_shape=jax.ShapeDtypeStruct(value_field.shape, F32),
            in_specs=[pl.BlockSpec(memory_space=pltpu.HBM)] * 3,
            out_specs=pl.BlockSpec(memory_space=pltpu.VMEM),
            scratch_shapes=[
                pltpu.VMEM((4, 12, 8, 128), F32),
                pltpu.VMEM((4, 8, 8, 128), F32),
                pltpu.VMEM((4, 12, 8, 128), F32),
                pltpu.VMEM((4, 8, 8, 128), F32),
                pltpu.VMEM((4, 8, 8, 128), F32),
                pltpu.VMEM((4, 4, 8, 128), F32),
                pltpu.VMEM((4, 8, 8, 128), F32),
                pltpu.VMEM((4, 8, 8, 128), F32),
                pltpu.VMEM((4, 8, 8, 128), F32),
                pltpu.VMEM((2, 2, 8, 128), jnp.int32),
                pltpu.VMEM((2, 2, 8, 8, 128), F32),
                pltpu.VMEM((4, 128), jnp.int32),
                pltpu.VMEM((n_gx, 4, 128), F32),
                pltpu.VMEM((2, 2, 4, 8, 128), F32),
                pltpu.SemaphoreType.DMA((18,)),
                pltpu.SemaphoreType.DMA((18,)),
                pltpu.SemaphoreType.DMA((n_gx - 1,)),
                pltpu.SemaphoreType.DMA((n_gx - 1,)),
                pltpu.SemaphoreType.DMA((4,)),
            ],
            compiler_params=pltpu.CompilerParams(collective_id=0, has_side_effects=True, vmem_limit_bytes=8 * 1024 * 1024),
            name="reach",
        )(*[pltpu.with_memory_space_constraint(x, pltpu.HBM) for x in (value_field, wind_grid, obstacle)])

    placed = (P(None, "gx", "ha", None), P(None, None, "gx", None), P("gx", None))
    return jax.shard_map(
        local, mesh=mesh, in_specs=placed, out_specs=P(None, "gx", "ha", None), check_vma=False
    )
```

```python
import functools
import math

import jax
import jax.numpy as jnp
from jax import lax
from jax.experimental import pallas as pl
from jax.experimental.pallas import tpu as pltpu
from jax.sharding import PartitionSpec as P

MESH = pl.DeviceIdType.MESH
STEPS = 2
TURN_RATE = 0.25
ACCEL_MAX = 0.5
SPEED_BASE = 0.5
SPEED_STEP = 0.25
SPEED_MAX = 1.25
WIND_SCALE = 1.0 / 512.0
CFL_NUMBER = 0.8
OBSTACLE_LEVEL = 1.0
F32 = jnp.float32


def limiter(before, here):
    return jnp.maximum(jnp.minimum(before, jnp.maximum(here, 0.0)), jnp.minimum(here, 0.0))


def parts(diff0, diff1, diff2, diff3):
    curve = diff2 - diff1
    backward = diff1 + 0.5 * limiter(diff1 - diff0, curve)
    forward = diff2 - 0.5 * limiter(curve, diff3 - diff2)
    return backward, forward


def plane_parts(values):
    n = values.shape[1] - 4
    diff = values[:, 1:] - values[:, :-1]
    curve = diff[:, 1:] - diff[:, :-1]
    limited = 0.5 * limiter(curve[:, :-1], curve[:, 1:])
    inner = diff[:, 1 : n + 2]
    return inner[:, :n] + limited[:, :n], inner[:, 1:] - limited[:, 1:]


def lane_parts(here):
    axis, extent = here.ndim - 1, here.shape[-1]
    lanes = lax.broadcasted_iota(jnp.int32, here.shape, axis)
    low1, low2 = pltpu.roll(here, 1, axis), pltpu.roll(here, 2, axis)
    up1, up2 = pltpu.roll(here, extent - 1, axis), pltpu.roll(here, extent - 2, axis)
    below, above = here - low1, up1 - here
    diff1 = jnp.where(lanes == 0, above, below)
    diff2 = jnp.where(lanes == extent - 1, below, above)
    diff0 = jnp.where(lanes <= 1, diff1, low1 - low2)
    diff3 = jnp.where(lanes >= extent - 2, diff2, up2 - up1)
    return parts(diff0, diff1, diff2, diff3)


def heading_term(here, other):
    axis = here.ndim - 2
    rows = lax.broadcasted_iota(jnp.int32, here.shape, axis)
    low2 = pltpu.roll(jnp.where(rows >= 6, other, here), 2, axis)
    low1 = pltpu.roll(jnp.where(rows == 7, other, here), 1, axis)
    up1 = pltpu.roll(jnp.where(rows == 0, other, here), 7, axis)
    up2 = pltpu.roll(jnp.where(rows <= 1, other, here), 6, axis)
    backward, forward = parts(low1 - low2, here - low1, up1 - here, up2 - up1)
    return jnp.maximum(backward, -forward)


def speed_terms(values):
    diff = [values[i + 1] - values[i] for i in range(3)]
    limited = 0.5 * limiter(diff[1] - diff[0], diff[2] - diff[1])
    return jnp.stack([
        jnp.abs(diff[0]),
        jnp.maximum(diff[0], limited - diff[1]),
        jnp.maximum(diff[1] + limited, -diff[2]),
        jnp.abs(diff[2]),
    ])


def kernel(
    n_gx, n_ha, field_hbm, wind_hbm, obstacle_hbm, out_v,
    v_a, w_a, v_b, w_b, sec_t, sec_w, known, jump_x, jump_y, wind_int, wind_f, obst, peaks, drift,
    send_sem, recv_sem, wind_send, wind_recv, ready, local_sem,
):
    gx, ha = lax.axis_index("gx"), lax.axis_index("ha")
    head_step = 2.0 * math.pi / (8 * n_ha)

    loads = [
        pltpu.make_async_copy(wind_hbm, wind_int.at[:, :, 2:6], local_sem.at[0]),
        pltpu.make_async_copy(field_hbm.at[:, :, 0:4], v_a.at[:, 4:8, 4:8], local_sem.at[1]),
        pltpu.make_async_copy(field_hbm.at[:, :, 4:8], w_a.at[:, 2:6, 0:4], local_sem.at[2]),
        pltpu.make_async_copy(obstacle_hbm, obst, local_sem.at[3]),
    ]
    for copy in loads:
        copy.start()

    def has(dx):
        return (gx + dx >= 0) & (gx + dx < n_gx)

    below, above = lax.rem(ha + n_ha - 1, n_ha), lax.rem(ha + 1, n_ha)
    barrier = pltpu.get_barrier_semaphore()

    def signal(semaphore, x, h):
        pl.semaphore_signal(semaphore, inc=1, device_id=(x, h), device_id_type=MESH)

    signal(barrier, gx, below)
    for dx in (1, -1):
        pl.when(has(dx))(functools.partial(signal, barrier, gx + dx, below))

    @pl.loop(gx + 1, n_gx)
    def _(k):
        signal(barrier, k, ha)

    loads[0].wait()
    for step in range(STEPS):
        for part in range(2):
            own = jnp.abs(wind_int[step, part, 2:6, :].astype(F32) * WIND_SCALE)
            peaks[gx, pl.ds(2 * step + part, 1), :] = jnp.max(own, axis=0, keepdims=True)
    rows = lax.broadcasted_iota(jnp.int32, (8, 128), 0)
    total = 8 * n_ha
    for tile in range(2):
        place = rows if tile == 0 else jnp.where(rows < 4, rows + 8, rows - 8)
        for step in range(STEPS):
            angle = lax.rem(ha * 8 + place + (total - 4 + 4 * step), total).astype(F32) * head_step
            for part, value in enumerate((jnp.cos(angle), jnp.sin(angle))):
                for s in range(4):
                    drift[step, tile, part, s] = (SPEED_BASE + SPEED_STEP * s) * value
    loads[1].wait()
    loads[2].wait()

    pl.semaphore_wait(
        barrier, 1 + gx + has(1).astype(jnp.int32) + has(-1).astype(jnp.int32)
    )

    def remote(src, dst, index, dx, dh):
        return pltpu.make_async_remote_copy(
            src_ref=src, dst_ref=dst, send_sem=send_sem.at[index], recv_sem=recv_sem.at[index],
            device_id=(gx + dx, lax.rem(ha + dh + n_ha, n_ha)), device_id_type=MESH,
        )

    def halo(v, w, base, way):
        low, high = slice(0, 4), slice(4, 8)
        mine, theirs = (high, low) if way > 0 else (low, high)
        inner, outer = (slice(0, 2), slice(6, 8)) if way > 0 else (slice(6, 8), slice(0, 2))
        copies, sides = [], ((1, slice(0, 4), slice(6, 8), slice(0, 2)), (-1, slice(8, 12), slice(4, 6), slice(6, 8)))
        for dx, to, near, far in sides:
            near_w = slice(near.start - 2, near.stop - 2)
            copies += [
                (dx, v.at[:, near, outer], w.at[:, far, outer], way),
                (dx, w.at[:, 2:6, theirs], v.at[:, to, theirs], way),
                (dx, w.at[:, near_w, inner], w.at[:, far, inner], 0),
                (dx, v.at[:, 4:8, mine], v.at[:, to, mine], 0),
            ]
        copies = [copies[n] for n in (0, 4, 1, 5)] + [
            (0, w.at[:, 2:6, theirs], v.at[:, 4:8, theirs], way),
            (0, v.at[:, 4:8, mine], w.at[:, 2:6, mine], way),
        ] + [copies[n] for n in (2, 6, 3, 7)]
        return [
            (dx, remote(src, dst, base + n, dx, dh)) for n, (dx, src, dst, dh) in enumerate(copies)
        ]

    def start(copies):
        for dx in (0, 1, -1):
            mine = [copy for d, copy in copies if d == dx]

            def run(mine=mine):
                for copy in mine:
                    copy.start()

            guarded(dx, mine, run)

    def receive(copies):
        for dx in (0, 1, -1):
            mine = [copy for d, copy in copies if d == dx]

            def run(mine=mine):
                for copy in mine:
                    copy.wait_recv()

            guarded(-dx, mine, run)

    def finish_sends(copies):
        for dx in (0, 1, -1):
            mine = [copy for d, copy in copies if d == dx]

            def run(mine=mine):
                for copy in mine:
                    copy.wait_send()

            guarded(dx, mine, run)

    def guarded(dx, mine, run):
        if not mine:
            return
        if dx == 0:
            run()
        else:
            pl.when(has(dx))(run)

    first = halo(v_a, w_a, 0, 1)
    second = halo(v_b, w_b, 10, -1)
    wind_edges = [
        (1, remote(wind_int.at[:, :, 4:6], wind_int.at[:, :, 0:2], 20, 1, 0)),
        (-1, remote(wind_int.at[:, :, 2:4], wind_int.at[:, :, 6:8], 21, -1, 0)),
    ]
    def wind_copy(k):
        return pltpu.make_async_remote_copy(
            src_ref=peaks.at[gx], dst_ref=peaks.at[gx], send_sem=wind_send.at[k], recv_sem=wind_recv.at[gx],
            device_id=(k, ha), device_id_type=MESH,
        )

    def wind_arrival(k):
        return pltpu.make_async_remote_copy(
            src_ref=peaks.at[k], dst_ref=peaks.at[k], send_sem=wind_send.at[k], recv_sem=wind_recv.at[k],
            device_id=(k, ha), device_id_type=MESH,
        )

    pl.when(has(-1))(lambda: signal(ready.at[0], gx - 1, ha))

    @pl.loop(0, gx)
    def _(k):
        signal(ready.at[1], k, ha)

    upward = [copy for n, copy in enumerate(first) if n in (6, 8)] + wind_edges[:1]
    start(first[:6])
    start([copy for n, copy in enumerate(first) if n in (7, 9)] + wind_edges[1:])

    @pl.loop(0, gx)
    def _(k):
        wind_copy(k).start()

    half_scale = ACCEL_MAX / SPEED_STEP * 2.0
    head_scale = 2.0 * TURN_RATE / head_step
    own, left, right = slice(4, 8), slice(2, 4), slice(8, 10)

    def ends(ref, low, count):
        for at_end, edge, next_one, near, far in (
            (gx == 0, low, low + 1, low - 1, low - 2),
            (gx == n_gx - 1, low + count - 1, low + count - 2, low + count, low + count + 1),
        ):
            a, b = ref[:, edge], ref[:, next_one]
            ref[:, near] = jnp.where(at_end, 2.0 * a - b, ref[:, near])
            ref[:, far] = jnp.where(at_end, 3.0 * a - 2.0 * b, ref[:, far])

    def across(step, tile, planes, here):
        back, fore = lane_parts(here)
        velocity = drift[step, tile, 1][:, None] + wind_f[step, 1, planes][None]
        return (back + fore) * velocity, fore - back

    def along(step, tile, planes, around):
        back, fore = plane_parts(around)
        velocity = drift[step, tile, 0][:, None] + wind_f[step, 0, planes][None]
        return (back + fore) * velocity, fore - back

    def begin(step, v, planes):
        place = slice(planes.start - 2, planes.stop - 2)
        values = v[:, planes]
        mean, jump = across(step, 0, place, values)
        known[:, place] = mean - half_scale * speed_terms(values)
        jump_y[:, place] = jump

    def extend_x(step, v):
        for block in (0, 4):
            place = slice(block, block + 4)
            mean, jump = along(step, 0, place, v[:, block : block + 8])
            known[:, place] = known[:, place] + mean
            jump_x[:, place] = jump

    def whole(step, tile, planes, around, here, other):
        alpha_x, alpha_y = alphas[step]
        mean_x, jump_at_x = along(step, tile, planes, around)
        mean_y, jump_at_y = across(step, tile, planes, here)
        result = mean_x + mean_y + alpha_x * jump_at_x + alpha_y * jump_at_y
        return halves[step] * (
            result - head_scale * heading_term(here, other) - half_scale * speed_terms(here)
        )

    def first_stage(step, v, w):
        alpha_x, alpha_y = alphas[step]
        for block in (0, 4):
            place = slice(block, block + 4)
            here, other = v[:, block + 2 : block + 6], w[:, place]
            rest = known[:, place] + alpha_x * jump_x[:, place] + alpha_y * jump_y[:, place]
            sec_t[:, place] = here + halves[step] * (rest - head_scale * heading_term(here, other))
        here = w[:, 2:6]
        sec_w[...] = here + whole(step, 1, slice(2, 6), w[...], here, v[:, own])

    def second_stage(step, v, finish):
        ends(sec_t, 2, 4)
        here = sec_t[:, 2:6]
        change = whole(step, 0, slice(2, 6), sec_t[...], here, sec_w[...])
        finish(0.5 * (v[:, own] + (here + change)))

    def limit(candidate, plane):
        blocked = jnp.broadcast_to(obst[pl.ds(plane, 1), :], (8, 128)) == 1
        value = candidate[:, plane]
        return jnp.where(blocked[None], jnp.maximum(value, OBSTACLE_LEVEL), value)

    def keep(candidate):
        for plane in range(4):
            swapped = pltpu.roll(limit(candidate, plane), 4, 1)
            v_b[:, 4 + plane, 0:4] = swapped[:, 0:4]
            w_b[:, 2 + plane, 4:8] = swapped[:, 4:8]
        start(second)

    def give(candidate):
        for plane in range(4):
            out_v[:, plane] = limit(candidate, plane)

    def spread(planes):
        for step in range(STEPS):
            for part in range(2):
                for plane in planes:
                    row = wind_int[step, part, pl.ds(plane, 1), :].astype(F32) * WIND_SCALE
                    wind_f[step, part, plane] = jnp.broadcast_to(row, (8, 128))

    spread(range(2, 6))

    @pl.when(has(1))
    def _():
        pl.semaphore_wait(ready.at[0], 1)

    start(upward)

    @pl.when(gx < n_gx - 1)
    def _():
        pl.semaphore_wait(ready.at[1], n_gx - 1 - gx)

    @pl.loop(gx + 1, n_gx)
    def _(k):
        wind_copy(k).start()

    receive(wind_edges)
    spread((0, 1, 6, 7))

    loads[3].wait()
    receive(first[4:6])
    begin(0, v_a, own)
    receive(first[:4] + first[6:])
    ends(v_a, 4, 4)
    ends(w_a, 2, 4)
    begin(0, v_a, left)
    begin(0, v_a, right)
    extend_x(0, v_a)

    @pl.loop(0, n_gx - 1)
    def _(n):
        wind_arrival(n + (n >= gx).astype(jnp.int32)).wait_recv()

    highest = jnp.max(peaks[...], axis=0)
    highest = jnp.max(highest, axis=1, keepdims=True)
    alphas, halves = [], []
    for step in range(STEPS):
        pair = [
            jnp.broadcast_to(SPEED_MAX + highest[2 * step + part : 2 * step + part + 1], (8, 128))
            for part in range(2)
        ]
        alphas.append(pair)
        halves.append(
            (0.5 * CFL_NUMBER)
            / (pair[0] + pair[1] + (TURN_RATE / head_step + ACCEL_MAX / SPEED_STEP))
        )

    first_stage(0, v_a, w_a)
    second_stage(0, v_a, keep)

    receive(second[4:6])
    begin(1, v_b, own)
    receive(second[:4] + second[6:])
    ends(v_b, 4, 4)
    ends(w_b, 2, 4)
    begin(1, v_b, left)
    begin(1, v_b, right)
    extend_x(1, v_b)
    first_stage(1, v_b, w_b)
    second_stage(1, v_b, give)
    finish_sends(first + wind_edges + second)

    @pl.loop(0, n_gx - 1)
    def _(n):
        wind_arrival(n + (n >= gx).astype(jnp.int32)).wait_send()


def solution(mesh):
    n_gx, n_ha = mesh.shape["gx"], mesh.shape["ha"]

    def local(value_field, wind_grid, obstacle):
        return pl.pallas_call(
            functools.partial(kernel, n_gx, n_ha),
            out_shape=jax.ShapeDtypeStruct(value_field.shape, F32),
            in_specs=[pl.BlockSpec(memory_space=pltpu.HBM)] * 3,
            out_specs=pl.BlockSpec(memory_space=pltpu.VMEM),
            scratch_shapes=[
                pltpu.VMEM((4, 12, 8, 128), F32),
                pltpu.VMEM((4, 8, 8, 128), F32),
                pltpu.VMEM((4, 12, 8, 128), F32),
                pltpu.VMEM((4, 8, 8, 128), F32),
                pltpu.VMEM((4, 8, 8, 128), F32),
                pltpu.VMEM((4, 4, 8, 128), F32),
                pltpu.VMEM((4, 8, 8, 128), F32),
                pltpu.VMEM((4, 8, 8, 128), F32),
                pltpu.VMEM((4, 8, 8, 128), F32),
                pltpu.VMEM((2, 2, 8, 128), jnp.int32),
                pltpu.VMEM((2, 2, 8, 8, 128), F32),
                pltpu.VMEM((4, 128), jnp.int32),
                pltpu.VMEM((n_gx, 4, 128), F32),
                pltpu.VMEM((2, 2, 2, 4, 8, 128), F32),
                pltpu.SemaphoreType.DMA((22,)),
                pltpu.SemaphoreType.DMA((22,)),
                pltpu.SemaphoreType.DMA((n_gx,)),
                pltpu.SemaphoreType.DMA((n_gx,)),
                pltpu.SemaphoreType.REGULAR((2,)),
                pltpu.SemaphoreType.DMA((4,)),
            ],
            compiler_params=pltpu.CompilerParams(collective_id=0, has_side_effects=True, vmem_limit_bytes=8 * 1024 * 1024),
            name="reach",
        )(*[pltpu.with_memory_space_constraint(x, pltpu.HBM) for x in (value_field, wind_grid, obstacle)])

    placed = (P(None, "gx", "ha", None), P(None, None, "gx", None), P("gx", None))
    return jax.shard_map(
        local, mesh=mesh, in_specs=placed, out_specs=P(None, "gx", "ha", None), check_vma=False
    )
```

```python
import functools
import math

import jax
import jax.numpy as jnp
from jax import lax
from jax.experimental import pallas as pl
from jax.experimental.pallas import tpu as pltpu
from jax.sharding import PartitionSpec as P

MESH = pl.DeviceIdType.MESH
STEPS = 2
TURN_RATE = 0.25
ACCEL_MAX = 0.5
SPEED_BASE = 0.5
SPEED_STEP = 0.25
SPEED_MAX = 1.25
WIND_SCALE = 1.0 / 512.0
CFL_NUMBER = 0.8
OBSTACLE_LEVEL = 1.0
F32 = jnp.float32


def limiter(before, here):
    return jnp.maximum(jnp.minimum(before, jnp.maximum(here, 0.0)), jnp.minimum(here, 0.0))


def parts(diff0, diff1, diff2, diff3):
    curve = diff2 - diff1
    backward = diff1 + 0.5 * limiter(diff1 - diff0, curve)
    forward = diff2 - 0.5 * limiter(curve, diff3 - diff2)
    return backward, forward


def plane_parts(values):
    n = values.shape[1] - 4
    diff = values[:, 1:] - values[:, :-1]
    curve = diff[:, 1:] - diff[:, :-1]
    limited = 0.5 * limiter(curve[:, :-1], curve[:, 1:])
    inner = diff[:, 1 : n + 2]
    return inner[:, :n] + limited[:, :n], inner[:, 1:] - limited[:, 1:]


def lane_parts(here):
    axis, extent = here.ndim - 1, here.shape[-1]
    lanes = lax.broadcasted_iota(jnp.int32, here.shape, axis)
    low1, low2 = pltpu.roll(here, 1, axis), pltpu.roll(here, 2, axis)
    up1, up2 = pltpu.roll(here, extent - 1, axis), pltpu.roll(here, extent - 2, axis)
    below, above = here - low1, up1 - here
    diff1 = jnp.where(lanes == 0, above, below)
    diff2 = jnp.where(lanes == extent - 1, below, above)
    diff0 = jnp.where(lanes <= 1, diff1, low1 - low2)
    diff3 = jnp.where(lanes >= extent - 2, diff2, up2 - up1)
    return parts(diff0, diff1, diff2, diff3)


def heading_term(here, other):
    axis = here.ndim - 2
    rows = lax.broadcasted_iota(jnp.int32, here.shape, axis)
    low2 = pltpu.roll(jnp.where(rows >= 6, other, here), 2, axis)
    low1 = pltpu.roll(jnp.where(rows == 7, other, here), 1, axis)
    up1 = pltpu.roll(jnp.where(rows == 0, other, here), 7, axis)
    up2 = pltpu.roll(jnp.where(rows <= 1, other, here), 6, axis)
    backward, forward = parts(low1 - low2, here - low1, up1 - here, up2 - up1)
    return jnp.maximum(backward, -forward)


def speed_terms(values):
    diff = [values[i + 1] - values[i] for i in range(3)]
    limited = 0.5 * limiter(diff[1] - diff[0], diff[2] - diff[1])
    return jnp.stack([
        jnp.abs(diff[0]),
        jnp.maximum(diff[0], limited - diff[1]),
        jnp.maximum(diff[1] + limited, -diff[2]),
        jnp.abs(diff[2]),
    ])


def kernel(
    n_gx, n_ha, field_hbm, wind_hbm, obstacle_hbm, out_v,
    v_a, w_a, v_b, w_b, sec_t, sec_w, known, jump_x, jump_y, wind_int, wind_f, obst, peaks, drift,
    send_sem, recv_sem, wind_send, wind_recv, ready, local_sem,
):
    gx, ha = lax.axis_index("gx"), lax.axis_index("ha")
    head_step = 2.0 * math.pi / (8 * n_ha)

    loads = [
        pltpu.make_async_copy(wind_hbm, wind_int.at[:, :, 2:6], local_sem.at[0]),
        pltpu.make_async_copy(field_hbm.at[:, :, 0:4], v_a.at[:, 4:8, 4:8], local_sem.at[1]),
        pltpu.make_async_copy(field_hbm.at[:, :, 4:8], w_a.at[:, 2:6, 0:4], local_sem.at[2]),
        pltpu.make_async_copy(obstacle_hbm, obst, local_sem.at[3]),
    ]
    for copy in loads:
        copy.start()

    def has(dx):
        return (gx + dx >= 0) & (gx + dx < n_gx)

    below, above = lax.rem(ha + n_ha - 1, n_ha), lax.rem(ha + 1, n_ha)
    barrier = pltpu.get_barrier_semaphore()

    def signal(semaphore, x, h):
        pl.semaphore_signal(semaphore, inc=1, device_id=(x, h), device_id_type=MESH)

    signal(barrier, gx, below)
    for dx in (1, -1):
        pl.when(has(dx))(functools.partial(signal, barrier, gx + dx, below))

    @pl.loop(gx + 1, n_gx)
    def _(k):
        signal(barrier, k, ha)

    loads[1].wait()
    loads[2].wait()
    pl.semaphore_wait(
        barrier, 1 + gx + has(1).astype(jnp.int32) + has(-1).astype(jnp.int32)
    )

    def remote(src, dst, index, dx, dh):
        return pltpu.make_async_remote_copy(
            src_ref=src, dst_ref=dst, send_sem=send_sem.at[index], recv_sem=recv_sem.at[index],
            device_id=(gx + dx, lax.rem(ha + dh + n_ha, n_ha)), device_id_type=MESH,
        )

    def halo(v, w, base, way):
        low, high = slice(0, 4), slice(4, 8)
        mine, theirs = (high, low) if way > 0 else (low, high)
        inner, outer = (slice(0, 2), slice(6, 8)) if way > 0 else (slice(6, 8), slice(0, 2))

        copies, sides = [], ((1, slice(0, 4), slice(6, 8), slice(0, 2)), (-1, slice(8, 12), slice(4, 6), slice(6, 8)))
        for dx, to, near, far in sides:
            near_w = slice(near.start - 2, near.stop - 2)
            copies += [
                (dx, v.at[:, near, outer], w.at[:, far, outer], way),
                (dx, w.at[:, 2:6, theirs], v.at[:, to, theirs], way),
                (dx, w.at[:, near_w, inner], w.at[:, far, inner], 0),
                (dx, v.at[:, 4:8, mine], v.at[:, to, mine], 0),
            ]
        copies = [copies[n] for n in (0, 4, 1, 5)] + [
            (0, w.at[:, 2:6, theirs], v.at[:, 4:8, theirs], way),
            (0, v.at[:, 4:8, mine], w.at[:, 2:6, mine], way),
        ] + [copies[n] for n in (2, 6, 3, 7)]
        made = [
            (dx, remote(src, dst, base + n, dx, dh)) for n, (dx, src, dst, dh) in enumerate(copies)
        ]
        relays = [
            (-1, remote(w.at[:, 2:4, outer], w.at[:, 6:8, outer], base + 1, -1, 0)),
            (-1, remote(v.at[:, 4:8, theirs], v.at[:, 8:12, theirs], base + 3, -1, 0)),
        ]
        return made, relays

    odd = lax.rem(gx, 2) == 1

    def depart(copies):
        @pl.when(has(-1) & jnp.logical_not(odd))
        def _():
            copies[1][1].start()
            copies[3][1].start()

        start([copies[0], copies[2]] + copies[4:6])

    def relay(copies):
        @pl.when(odd)
        def _():
            for _, copy in copies:
                copy.start()

    def start(copies):
        for dx in (0, 1, -1):
            mine = [copy for d, copy in copies if d == dx]

            def run(mine=mine):
                for copy in mine:
                    copy.start()

            guarded(dx, mine, run)

    def receive(copies):
        for dx in (0, 1, -1):
            mine = [copy for d, copy in copies if d == dx]

            def run(mine=mine):
                for copy in mine:
                    copy.wait_recv()

            guarded(-dx, mine, run)

    def finish_sends(copies):
        for dx in (0, 1, -1):
            mine = [copy for d, copy in copies if d == dx]

            def run(mine=mine):
                for copy in mine:
                    copy.wait_send()

            guarded(dx, mine, run)

    def guarded(dx, mine, run):
        if not mine:
            return
        if dx == 0:
            run()
        else:
            pl.when(has(dx))(run)

    first, first_relays = halo(v_a, w_a, 0, 1)
    second, second_relays = halo(v_b, w_b, 10, -1)
    wind_edges = [
        (1, remote(wind_int.at[:, :, 4:6], wind_int.at[:, :, 0:2], 20, 1, 0)),
        (-1, remote(wind_int.at[:, :, 2:4], wind_int.at[:, :, 6:8], 21, -1, 0)),
    ]
    def wind_copy(k):
        return pltpu.make_async_remote_copy(
            src_ref=peaks.at[gx], dst_ref=peaks.at[gx], send_sem=wind_send.at[k], recv_sem=wind_recv.at[gx],
            device_id=(k, ha), device_id_type=MESH,
        )

    def wind_arrival(k):
        return pltpu.make_async_remote_copy(
            src_ref=peaks.at[k], dst_ref=peaks.at[k], send_sem=wind_send.at[k], recv_sem=wind_recv.at[k],
            device_id=(k, ha), device_id_type=MESH,
        )

    pl.when(has(-1))(lambda: signal(ready.at[0], gx - 1, ha))

    @pl.loop(0, gx)
    def _(k):
        signal(ready.at[1], k, ha)

    upward = [copy for n, copy in enumerate(first) if n in (6, 8)] + wind_edges[:1]
    depart(first)
    start([copy for n, copy in enumerate(first) if n in (7, 9)])

    loads[0].wait()
    quarters = lax.broadcasted_iota(jnp.int32, (1, 128), 1) // 32
    packed = jnp.zeros((1, 128), F32)
    for step in range(STEPS):
        for part in range(2):
            mine = jnp.max(jnp.abs(wind_int[step, part, 2:6, :].astype(F32) * WIND_SCALE), axis=0, keepdims=True)
            mine = jnp.max(mine, axis=1, keepdims=True)
            packed = jnp.where(quarters == 2 * step + part, mine, packed)
    peaks[gx] = packed
    start(wind_edges[1:])

    @pl.loop(0, gx)
    def _(k):
        wind_copy(k).start()

    half_scale = ACCEL_MAX / SPEED_STEP * 2.0
    head_scale = 2.0 * TURN_RATE / head_step
    own, left, right = slice(4, 8), slice(2, 4), slice(8, 10)

    def ends(ref, low, count):
        for at_end, edge, next_one, near, far in (
            (gx == 0, low, low + 1, low - 1, low - 2),
            (gx == n_gx - 1, low + count - 1, low + count - 2, low + count, low + count + 1),
        ):
            a, b = ref[:, edge], ref[:, next_one]
            ref[:, near] = jnp.where(at_end, 2.0 * a - b, ref[:, near])
            ref[:, far] = jnp.where(at_end, 3.0 * a - 2.0 * b, ref[:, far])

    def across(step, tile, planes, here):
        back, fore = lane_parts(here)
        velocity = drift[step, tile, 1][:, None] + wind_f[step, 1, planes][None]
        return (back + fore) * velocity, fore - back

    def along(step, tile, planes, around):
        back, fore = plane_parts(around)
        velocity = drift[step, tile, 0][:, None] + wind_f[step, 0, planes][None]
        return (back + fore) * velocity, fore - back

    def begin(step, v, planes):
        place = slice(planes.start - 2, planes.stop - 2)
        values = v[:, planes]
        mean, jump = across(step, 0, place, values)
        known[:, place] = mean - half_scale * speed_terms(values)
        jump_y[:, place] = jump

    def extend_x(step, v):
        for block in (0, 4):
            place = slice(block, block + 4)
            mean, jump = along(step, 0, place, v[:, block : block + 8])
            known[:, place] = known[:, place] + mean
            jump_x[:, place] = jump

    def whole(step, tile, planes, around, here, other):
        alpha_x, alpha_y = alphas[step]
        mean_x, jump_at_x = along(step, tile, planes, around)
        mean_y, jump_at_y = across(step, tile, planes, here)
        result = mean_x + mean_y + alpha_x * jump_at_x + alpha_y * jump_at_y
        return halves[step] * (
            result - head_scale * heading_term(here, other) - half_scale * speed_terms(here)
        )

    def first_stage(step, v, w):
        alpha_x, alpha_y = alphas[step]
        for block in (0, 4):
            place = slice(block, block + 4)
            here, other = v[:, block + 2 : block + 6], w[:, place]
            rest = known[:, place] + alpha_x * jump_x[:, place] + alpha_y * jump_y[:, place]
            sec_t[:, place] = here + halves[step] * (rest - head_scale * heading_term(here, other))
        here = w[:, 2:6]
        sec_w[...] = here + whole(step, 1, slice(2, 6), w[...], here, v[:, own])

    def second_stage(step, v, finish):
        ends(sec_t, 2, 4)
        here = sec_t[:, 2:6]
        change = whole(step, 0, slice(2, 6), sec_t[...], here, sec_w[...])
        finish(0.5 * (v[:, own] + (here + change)))

    def limit(candidate, plane):
        blocked = jnp.broadcast_to(obst[pl.ds(plane, 1), :], (8, 128)) == 1
        value = candidate[:, plane]
        return jnp.where(blocked[None], jnp.maximum(value, OBSTACLE_LEVEL), value)

    def keep(candidate):
        for plane in range(4):
            swapped = pltpu.roll(limit(candidate, plane), 4, 1)
            v_b[:, 4 + plane, 0:4] = swapped[:, 0:4]
            w_b[:, 2 + plane, 4:8] = swapped[:, 4:8]
        depart(second)
        start(second[6:])

    def give(candidate):
        for plane in range(4):
            out_v[:, plane] = limit(candidate, plane)

    def spread(planes):
        for step in range(STEPS):
            for part in range(2):
                for plane in planes:
                    row = wind_int[step, part, pl.ds(plane, 1), :].astype(F32) * WIND_SCALE
                    wind_f[step, part, plane] = jnp.broadcast_to(row, (8, 128))

    spread(range(2, 6))
    rows = lax.broadcasted_iota(jnp.int32, (8, 128), 0)
    total = 8 * n_ha
    for tile in range(2):
        place = rows if tile == 0 else jnp.where(rows < 4, rows + 8, rows - 8)
        for step in range(STEPS):
            angle = lax.rem(ha * 8 + place + (total - 4 + 4 * step), total).astype(F32) * head_step
            for part, value in enumerate((jnp.cos(angle), jnp.sin(angle))):
                for s in range(4):
                    drift[step, tile, part, s] = (SPEED_BASE + SPEED_STEP * s) * value


    @pl.when(has(1))
    def _():
        pl.semaphore_wait(ready.at[0], 1)

    start(upward)

    @pl.when(gx < n_gx - 1)
    def _():
        pl.semaphore_wait(ready.at[1], n_gx - 1 - gx)

    @pl.loop(gx + 1, n_gx)
    def _(k):
        wind_copy(k).start()

    receive(wind_edges)
    spread((0, 1, 6, 7))

    loads[3].wait()
    receive(first[4:6])
    relay(first_relays)
    begin(0, v_a, own)
    receive(first[:4] + first[6:])
    ends(v_a, 4, 4)
    ends(w_a, 2, 4)
    begin(0, v_a, left)
    begin(0, v_a, right)
    extend_x(0, v_a)

    @pl.loop(0, n_gx - 1)
    def _(n):
        wind_arrival(n + (n >= gx).astype(jnp.int32)).wait_recv()

    highest = jnp.max(peaks[...], axis=0)
    quarters = lax.broadcasted_iota(jnp.int32, (1, 128), 1) // 32
    highest = [jnp.max(jnp.where(quarters == n, highest, 0.0), axis=1, keepdims=True) for n in range(4)]
    alphas, halves = [], []
    for step in range(STEPS):
        pair = [
            jnp.broadcast_to(SPEED_MAX + highest[2 * step + part], (8, 128))
            for part in range(2)
        ]
        alphas.append(pair)
        halves.append(
            (0.5 * CFL_NUMBER)
            / (pair[0] + pair[1] + (TURN_RATE / head_step + ACCEL_MAX / SPEED_STEP))
        )

    first_stage(0, v_a, w_a)
    second_stage(0, v_a, keep)

    receive(second[4:6])
    relay(second_relays)
    begin(1, v_b, own)
    receive(second[:4] + second[6:])
    ends(v_b, 4, 4)
    ends(w_b, 2, 4)
    begin(1, v_b, left)
    begin(1, v_b, right)
    extend_x(1, v_b)
    first_stage(1, v_b, w_b)
    second_stage(1, v_b, give)
    finish_sends(first + wind_edges + second)

    @pl.loop(0, n_gx - 1)
    def _(n):
        wind_arrival(n + (n >= gx).astype(jnp.int32)).wait_send()


def solution(mesh):
    n_gx, n_ha = mesh.shape["gx"], mesh.shape["ha"]

    def local(value_field, wind_grid, obstacle):
        return pl.pallas_call(
            functools.partial(kernel, n_gx, n_ha),
            out_shape=jax.ShapeDtypeStruct(value_field.shape, F32),
            in_specs=[pl.BlockSpec(memory_space=pltpu.HBM)] * 3,
            out_specs=pl.BlockSpec(memory_space=pltpu.VMEM),
            scratch_shapes=[
                pltpu.VMEM((4, 12, 8, 128), F32),
                pltpu.VMEM((4, 8, 8, 128), F32),
                pltpu.VMEM((4, 12, 8, 128), F32),
                pltpu.VMEM((4, 8, 8, 128), F32),
                pltpu.VMEM((4, 8, 8, 128), F32),
                pltpu.VMEM((4, 4, 8, 128), F32),
                pltpu.VMEM((4, 8, 8, 128), F32),
                pltpu.VMEM((4, 8, 8, 128), F32),
                pltpu.VMEM((4, 8, 8, 128), F32),
                pltpu.VMEM((2, 2, 8, 128), jnp.int32),
                pltpu.VMEM((2, 2, 8, 8, 128), F32),
                pltpu.VMEM((4, 128), jnp.int32),
                pltpu.VMEM((n_gx, 1, 128), F32),
                pltpu.VMEM((2, 2, 2, 4, 8, 128), F32),
                pltpu.SemaphoreType.DMA((22,)),
                pltpu.SemaphoreType.DMA((22,)),
                pltpu.SemaphoreType.DMA((n_gx,)),
                pltpu.SemaphoreType.DMA((n_gx,)),
                pltpu.SemaphoreType.REGULAR((2,)),
                pltpu.SemaphoreType.DMA((4,)),
            ],
            compiler_params=pltpu.CompilerParams(collective_id=0, has_side_effects=True, vmem_limit_bytes=8 * 1024 * 1024),
            name="reach",
        )(*[pltpu.with_memory_space_constraint(x, pltpu.HBM) for x in (value_field, wind_grid, obstacle)])

    placed = (P(None, "gx", "ha", None), P(None, None, "gx", None), P("gx", None))
    return jax.shard_map(
        local, mesh=mesh, in_specs=placed, out_specs=P(None, "gx", "ha", None), check_vma=False
    )
```

```python
import functools
import math

import jax
import jax.numpy as jnp
from jax import lax
from jax.experimental import pallas as pl
from jax.experimental.pallas import tpu as pltpu
from jax.sharding import PartitionSpec as P

MESH = pl.DeviceIdType.MESH
STEPS = 2
TURN_RATE = 0.25
ACCEL_MAX = 0.5
SPEED_BASE = 0.5
SPEED_STEP = 0.25
SPEED_MAX = 1.25
WIND_SCALE = 1.0 / 512.0
CFL_NUMBER = 0.8
OBSTACLE_LEVEL = 1.0
F32 = jnp.float32


def limiter(before, here):
    return jnp.maximum(jnp.minimum(before, jnp.maximum(here, 0.0)), jnp.minimum(here, 0.0))


def parts(diff0, diff1, diff2, diff3):
    curve = diff2 - diff1
    backward = diff1 + 0.5 * limiter(diff1 - diff0, curve)
    forward = diff2 - 0.5 * limiter(curve, diff3 - diff2)
    return backward, forward


def plane_parts(values):
    n = values.shape[1] - 4
    diff = values[:, 1:] - values[:, :-1]
    curve = diff[:, 1:] - diff[:, :-1]
    limited = 0.5 * limiter(curve[:, :-1], curve[:, 1:])
    inner = diff[:, 1 : n + 2]
    return inner[:, :n] + limited[:, :n], inner[:, 1:] - limited[:, 1:]


def lane_parts(here):
    axis, extent = here.ndim - 1, here.shape[-1]
    lanes = lax.broadcasted_iota(jnp.int32, here.shape, axis)
    low1, low2 = pltpu.roll(here, 1, axis), pltpu.roll(here, 2, axis)
    up1, up2 = pltpu.roll(here, extent - 1, axis), pltpu.roll(here, extent - 2, axis)
    below, above = here - low1, up1 - here
    diff1 = jnp.where(lanes == 0, above, below)
    diff2 = jnp.where(lanes == extent - 1, below, above)
    diff0 = jnp.where(lanes <= 1, diff1, low1 - low2)
    diff3 = jnp.where(lanes >= extent - 2, diff2, up2 - up1)
    return parts(diff0, diff1, diff2, diff3)


def heading_term(here, other):
    axis = here.ndim - 2
    rows = lax.broadcasted_iota(jnp.int32, here.shape, axis)
    low2 = pltpu.roll(jnp.where(rows >= 6, other, here), 2, axis)
    low1 = pltpu.roll(jnp.where(rows == 7, other, here), 1, axis)
    up1 = pltpu.roll(jnp.where(rows == 0, other, here), 7, axis)
    up2 = pltpu.roll(jnp.where(rows <= 1, other, here), 6, axis)
    backward, forward = parts(low1 - low2, here - low1, up1 - here, up2 - up1)
    return jnp.maximum(backward, -forward)


def speed_terms(values):
    diff = [values[i + 1] - values[i] for i in range(3)]
    limited = 0.5 * limiter(diff[1] - diff[0], diff[2] - diff[1])
    return jnp.stack([
        jnp.abs(diff[0]),
        jnp.maximum(diff[0], limited - diff[1]),
        jnp.maximum(diff[1] + limited, -diff[2]),
        jnp.abs(diff[2]),
    ])


def kernel(
    n_gx, n_ha, field_hbm, wind_hbm, obstacle_hbm, out_v,
    v_a, w_a, v_b, w_b, sec_t, sec_w, known, jump_x, jump_y, wind_int, wind_f, obst, peaks, drift,
    send_sem, recv_sem, wind_send, wind_recv, ready, local_sem,
):
    gx, ha = lax.axis_index("gx"), lax.axis_index("ha")
    head_step = 2.0 * math.pi / (8 * n_ha)

    loads = [
        pltpu.make_async_copy(wind_hbm, wind_int.at[:, :, 2:6], local_sem.at[0]),
        pltpu.make_async_copy(field_hbm.at[:, :, 0:4], v_a.at[:, 4:8, 4:8], local_sem.at[1]),
        pltpu.make_async_copy(field_hbm.at[:, :, 4:8], w_a.at[:, 2:6, 0:4], local_sem.at[2]),
        pltpu.make_async_copy(obstacle_hbm, obst, local_sem.at[3]),
    ]
    for copy in loads:
        copy.start()

    def has(dx):
        return (gx + dx >= 0) & (gx + dx < n_gx)

    below, above = lax.rem(ha + n_ha - 1, n_ha), lax.rem(ha + 1, n_ha)
    barrier = pltpu.get_barrier_semaphore()

    def signal(semaphore, x, h):
        pl.semaphore_signal(semaphore, inc=1, device_id=(x, h), device_id_type=MESH)

    signal(barrier, gx, below)
    for dx in (1, -1):
        pl.when(has(dx))(functools.partial(signal, barrier, gx + dx, below))

    @pl.loop(gx + 1, n_gx)
    def _(k):
        signal(barrier, k, ha)

    loads[1].wait()
    loads[2].wait()
    pl.semaphore_wait(
        barrier, 1 + gx + has(1).astype(jnp.int32) + has(-1).astype(jnp.int32)
    )

    def remote(src, dst, index, dx, dh):
        return pltpu.make_async_remote_copy(
            src_ref=src, dst_ref=dst, send_sem=send_sem.at[index], recv_sem=recv_sem.at[index],
            device_id=(gx + dx, lax.rem(ha + dh + n_ha, n_ha)), device_id_type=MESH,
        )

    def halo(v, w, base, way):
        low, high = slice(0, 4), slice(4, 8)
        mine, theirs = (high, low) if way > 0 else (low, high)
        inner, outer = (slice(0, 2), slice(6, 8)) if way > 0 else (slice(6, 8), slice(0, 2))

        copies, sides = [], ((1, slice(0, 4), slice(6, 8), slice(0, 2)), (-1, slice(8, 12), slice(4, 6), slice(6, 8)))
        for dx, to, near, far in sides:
            near_w = slice(near.start - 2, near.stop - 2)
            copies += [
                (dx, v.at[:, near, outer], w.at[:, far, outer], way),
                (dx, w.at[:, 2:6, theirs], v.at[:, to, theirs], way),
                (dx, w.at[:, near_w, inner], w.at[:, far, inner], 0),
                (dx, v.at[:, 4:8, mine], v.at[:, to, mine], 0),
            ]
        copies = [copies[n] for n in (0, 4, 1, 5)] + [
            (0, w.at[:, 2:6, theirs], v.at[:, 4:8, theirs], way),
            (0, v.at[:, 4:8, mine], w.at[:, 2:6, mine], way),
        ] + [copies[n] for n in (2, 6, 3, 7)]
        made = [
            (dx, remote(src, dst, base + n, dx, dh)) for n, (dx, src, dst, dh) in enumerate(copies)
        ]
        relays = [
            (-1, remote(w.at[:, 2:4, outer], w.at[:, 6:8, outer], base + 1, -1, 0)),
            (-1, remote(v.at[:, 4:8, theirs], v.at[:, 8:12, theirs], base + 3, -1, 0)),
        ]
        return made, relays

    odd = lax.rem(gx, 2) == 1

    def depart(copies):
        @pl.when(has(-1) & jnp.logical_not(odd))
        def _():
            copies[1][1].start()
            copies[3][1].start()

        start([copies[0], copies[2]] + copies[4:6])

    def relay(copies):
        @pl.when(odd)
        def _():
            for _, copy in copies:
                copy.start()

    def start(copies):
        for dx in (0, 1, -1):
            mine = [copy for d, copy in copies if d == dx]

            def run(mine=mine):
                for copy in mine:
                    copy.start()

            guarded(dx, mine, run)

    def receive(copies):
        for dx in (0, 1, -1):
            mine = [copy for d, copy in copies if d == dx]

            def run(mine=mine):
                for copy in mine:
                    copy.wait_recv()

            guarded(-dx, mine, run)

    def finish_sends(copies):
        for dx in (0, 1, -1):
            mine = [copy for d, copy in copies if d == dx]

            def run(mine=mine):
                for copy in mine:
                    copy.wait_send()

            guarded(dx, mine, run)

    def guarded(dx, mine, run):
        if not mine:
            return
        if dx == 0:
            run()
        else:
            pl.when(has(dx))(run)

    first, first_relays = halo(v_a, w_a, 0, 1)
    second, second_relays = halo(v_b, w_b, 10, -1)
    wind_edges = [
        (1, remote(wind_int.at[:, :, 4:6], wind_int.at[:, :, 0:2], 20, 1, 0)),
        (-1, remote(wind_int.at[:, :, 2:4], wind_int.at[:, :, 6:8], 21, -1, 0)),
    ]
    def wind_copy(k):
        return pltpu.make_async_remote_copy(
            src_ref=peaks.at[gx], dst_ref=peaks.at[gx], send_sem=wind_send.at[k], recv_sem=wind_recv.at[gx],
            device_id=(k, ha), device_id_type=MESH,
        )

    def wind_arrival(k):
        return pltpu.make_async_remote_copy(
            src_ref=peaks.at[k], dst_ref=peaks.at[k], send_sem=wind_send.at[k], recv_sem=wind_recv.at[k],
            device_id=(k, ha), device_id_type=MESH,
        )

    upward = [copy for n, copy in enumerate(first) if n in (6, 8)] + wind_edges[:1]
    depart(first)
    pl.when(has(-1))(lambda: signal(ready.at[0], gx - 1, ha))
    start([copy for n, copy in enumerate(first) if n in (7, 9)])

    @pl.loop(0, gx)
    def _(k):
        signal(ready.at[1], k, ha)

    loads[0].wait()
    quarters = lax.broadcasted_iota(jnp.int32, (1, 128), 1) // 32
    packed = jnp.zeros((1, 128), F32)
    for step in range(STEPS):
        for part in range(2):
            mine = jnp.max(jnp.abs(wind_int[step, part, 2:6, :].astype(F32) * WIND_SCALE), axis=0, keepdims=True)
            mine = jnp.max(mine, axis=1, keepdims=True)
            packed = jnp.where(quarters == 2 * step + part, mine, packed)
    peaks[gx] = packed
    start(wind_edges[1:])

    @pl.loop(0, gx)
    def _(k):
        wind_copy(k).start()

    half_scale = ACCEL_MAX / SPEED_STEP * 2.0
    head_scale = 2.0 * TURN_RATE / head_step
    own = slice(4, 8)

    def ends(ref, low, count):
        for at_end, edge, next_one, near, far in (
            (gx == 0, low, low + 1, low - 1, low - 2),
            (gx == n_gx - 1, low + count - 1, low + count - 2, low + count, low + count + 1),
        ):
            a, b = ref[:, edge], ref[:, next_one]
            ref[:, near] = jnp.where(at_end, 2.0 * a - b, ref[:, near])
            ref[:, far] = jnp.where(at_end, 3.0 * a - 2.0 * b, ref[:, far])

    def across(step, tile, planes, here):
        back, fore = lane_parts(here)
        velocity = drift[step, tile, 1][:, None] + wind_f[step, 1, planes][None]
        return (back + fore) * velocity, fore - back

    def along(step, tile, planes, around):
        back, fore = plane_parts(around)
        velocity = drift[step, tile, 0][:, None] + wind_f[step, 0, planes][None]
        return (back + fore) * velocity, fore - back

    def begin(step, v, plane, count):
        place = pl.ds(plane - 2, count)
        values = v[:, pl.ds(plane, count)]
        mean, jump = across(step, 0, place, values)
        known[:, place] = mean - half_scale * speed_terms(values)
        jump_y[:, place] = jump

    def extend_x(step, v, block):
        place = pl.ds(block, 4)
        mean, jump = along(step, 0, place, v[:, pl.ds(block, 8)])
        known[:, place] = known[:, place] + mean
        jump_x[:, place] = jump

    def whole(step, tile, planes, around, here, other):
        alpha_x, alpha_y = alphas[step]
        mean_x, jump_at_x = along(step, tile, planes, around)
        mean_y, jump_at_y = across(step, tile, planes, here)
        result = mean_x + mean_y + alpha_x * jump_at_x + alpha_y * jump_at_y
        return halves[step] * (
            result - head_scale * heading_term(here, other) - half_scale * speed_terms(here)
        )

    def first_stage(step, v, w, block):
        alpha_x, alpha_y = alphas[step]
        place = pl.ds(block, 4)
        here, other = v[:, pl.ds(block + 2, 4)], w[:, place]
        rest = known[:, place] + alpha_x * jump_x[:, place] + alpha_y * jump_y[:, place]
        sec_t[:, place] = here + halves[step] * (rest - head_scale * heading_term(here, other))

    def wings(step, v, w, plane, count):
        planes = pl.ds(plane, count)
        here, beside = w[:, planes], v[:, pl.ds(plane + 2, count)]
        change = whole(step, 1, planes, w[:, pl.ds(plane - 2, count + 4)], here, beside)
        sec_w[:, pl.ds(plane - 2, count)] = here + change

    def second_stage(step, v, finish):
        ends(sec_t, 2, 4)
        here = sec_t[:, 2:6]
        change = whole(step, 0, pl.ds(2, 4), sec_t[...], here, sec_w[...])
        finish(0.5 * (v[:, own] + (here + change)))

    def limit(candidate, plane):
        blocked = jnp.broadcast_to(obst[pl.ds(plane, 1), :], (8, 128)) == 1
        value = candidate[:, plane]
        return jnp.where(blocked[None], jnp.maximum(value, OBSTACLE_LEVEL), value)

    def keep(candidate):
        for plane in range(4):
            swapped = pltpu.roll(limit(candidate, plane), 4, 1)
            v_b[:, 4 + plane, 0:4] = swapped[:, 0:4]
            w_b[:, 2 + plane, 4:8] = swapped[:, 4:8]
        start(second[6:])
        depart(second)

    def give(candidate):
        for plane in range(4):
            out_v[:, plane] = limit(candidate, plane)

    def spread(planes):
        for step in range(STEPS):
            for part in range(2):
                for plane in planes:
                    row = wind_int[step, part, pl.ds(plane, 1), :].astype(F32) * WIND_SCALE
                    wind_f[step, part, plane] = jnp.broadcast_to(row, (8, 128))

    spread(range(2, 6))
    rows = lax.broadcasted_iota(jnp.int32, (8, 128), 0)
    total = 8 * n_ha
    for tile in range(2):
        place = rows if tile == 0 else jnp.where(rows < 4, rows + 8, rows - 8)
        for step in range(STEPS):
            angle = lax.rem(ha * 8 + place + (total - 4 + 4 * step), total).astype(F32) * head_step
            for part, value in enumerate((jnp.cos(angle), jnp.sin(angle))):
                for s in range(4):
                    drift[step, tile, part, s] = (SPEED_BASE + SPEED_STEP * s) * value


    @pl.when(has(1))
    def _():
        pl.semaphore_wait(ready.at[0], 1)

    start(upward)

    @pl.when(gx < n_gx - 1)
    def _():
        pl.semaphore_wait(ready.at[1], n_gx - 1 - gx)

    @pl.loop(gx + 1, n_gx)
    def _(k):
        wind_copy(k).start()

    receive(wind_edges)
    spread((0, 1, 6, 7))

    loads[3].wait()
    receive(first[4:6])
    relay(first_relays)
    begin(0, v_a, 4, 4)
    receive(first[:4] + first[6:])

    @pl.loop(0, n_gx - 1)
    def _(n):
        wind_arrival(n + (n >= gx).astype(jnp.int32)).wait_recv()

    ends(v_a, 4, 4)
    ends(w_a, 2, 4)
    begin(0, v_a, 2, 2)
    begin(0, v_a, 8, 2)
    extend_x(0, v_a, 0)
    extend_x(0, v_a, 4)

    highest = jnp.max(peaks[...], axis=0)
    quarters = lax.broadcasted_iota(jnp.int32, (1, 128), 1) // 32
    highest = [jnp.max(jnp.where(quarters == n, highest, 0.0), axis=1, keepdims=True) for n in range(4)]
    alphas, halves = [], []
    for step in range(STEPS):
        pair = [
            jnp.broadcast_to(SPEED_MAX + highest[2 * step + part], (8, 128))
            for part in range(2)
        ]
        alphas.append(pair)
        halves.append(
            (0.5 * CFL_NUMBER)
            / (pair[0] + pair[1] + (TURN_RATE / head_step + ACCEL_MAX / SPEED_STEP))
        )

    first_stage(0, v_a, w_a, 0)
    first_stage(0, v_a, w_a, 4)
    wings(0, v_a, w_a, 2, 4)
    second_stage(0, v_a, keep)

    receive(second[4:6])
    relay(second_relays)
    begin(1, v_b, 4, 4)

    parity = odd.astype(jnp.int32)
    near, far = 4 - 4 * parity, 4 * parity

    def side(copies, left):
        for copy in [copy for dx, copy in copies if dx == (1 if left else -1)]:
            copy.wait_recv()

    pl.when(odd)(functools.partial(side, second, True))
    pl.when(jnp.logical_not(odd))(functools.partial(side, second, False))
    begin(1, v_b, 2 + near + near // 2, 2)
    extend_x(1, v_b, near)
    first_stage(1, v_b, w_b, near)
    wings(1, v_b, w_b, 2 + near // 2, 2)
    pl.when(odd & has(1))(functools.partial(side, second, False))
    pl.when(jnp.logical_not(odd) & has(-1))(functools.partial(side, second, True))
    ends(v_b, 4, 4)
    ends(w_b, 2, 4)
    begin(1, v_b, 2 + far + far // 2, 2)
    extend_x(1, v_b, far)
    first_stage(1, v_b, w_b, far)
    wings(1, v_b, w_b, 2 + far // 2, 2)
    second_stage(1, v_b, give)
    finish_sends(first + wind_edges + second)

    @pl.loop(0, n_gx - 1)
    def _(n):
        wind_arrival(n + (n >= gx).astype(jnp.int32)).wait_send()


def solution(mesh):
    n_gx, n_ha = mesh.shape["gx"], mesh.shape["ha"]

    def local(value_field, wind_grid, obstacle):
        return pl.pallas_call(
            functools.partial(kernel, n_gx, n_ha),
            out_shape=jax.ShapeDtypeStruct(value_field.shape, F32),
            in_specs=[pl.BlockSpec(memory_space=pltpu.HBM)] * 3,
            out_specs=pl.BlockSpec(memory_space=pltpu.VMEM),
            scratch_shapes=[
                pltpu.VMEM((4, 12, 8, 128), F32),
                pltpu.VMEM((4, 8, 8, 128), F32),
                pltpu.VMEM((4, 12, 8, 128), F32),
                pltpu.VMEM((4, 8, 8, 128), F32),
                pltpu.VMEM((4, 8, 8, 128), F32),
                pltpu.VMEM((4, 4, 8, 128), F32),
                pltpu.VMEM((4, 8, 8, 128), F32),
                pltpu.VMEM((4, 8, 8, 128), F32),
                pltpu.VMEM((4, 8, 8, 128), F32),
                pltpu.VMEM((2, 2, 8, 128), jnp.int32),
                pltpu.VMEM((2, 2, 8, 8, 128), F32),
                pltpu.VMEM((4, 128), jnp.int32),
                pltpu.VMEM((n_gx, 1, 128), F32),
                pltpu.VMEM((2, 2, 2, 4, 8, 128), F32),
                pltpu.SemaphoreType.DMA((22,)),
                pltpu.SemaphoreType.DMA((22,)),
                pltpu.SemaphoreType.DMA((n_gx,)),
                pltpu.SemaphoreType.DMA((n_gx,)),
                pltpu.SemaphoreType.REGULAR((2,)),
                pltpu.SemaphoreType.DMA((4,)),
            ],
            compiler_params=pltpu.CompilerParams(collective_id=0, has_side_effects=True, vmem_limit_bytes=8 * 1024 * 1024),
            name="reach",
        )(*[pltpu.with_memory_space_constraint(x, pltpu.HBM) for x in (value_field, wind_grid, obstacle)])

    placed = (P(None, "gx", "ha", None), P(None, None, "gx", None), P("gx", None))
    return jax.shard_map(
        local, mesh=mesh, in_specs=placed, out_specs=P(None, "gx", "ha", None), check_vma=False
    )
```

```python
import functools
import math

import jax
import jax.numpy as jnp
from jax import lax
from jax.experimental import pallas as pl
from jax.experimental.pallas import tpu as pltpu
from jax.sharding import PartitionSpec as P

MESH = pl.DeviceIdType.MESH
STEPS = 2
TURN_RATE = 0.25
ACCEL_MAX = 0.5
SPEED_BASE = 0.5
SPEED_STEP = 0.25
SPEED_MAX = 1.25
WIND_SCALE = 1.0 / 512.0
CFL_NUMBER = 0.8
OBSTACLE_LEVEL = 1.0
F32 = jnp.float32


def limiter(before, here):
    return jnp.maximum(jnp.minimum(before, jnp.maximum(here, 0.0)), jnp.minimum(here, 0.0))


def parts(diff0, diff1, diff2, diff3):
    curve = diff2 - diff1
    backward = diff1 + 0.5 * limiter(diff1 - diff0, curve)
    forward = diff2 - 0.5 * limiter(curve, diff3 - diff2)
    return backward, forward


def plane_parts(values):
    n = values.shape[1] - 4
    diff = values[:, 1:] - values[:, :-1]
    curve = diff[:, 1:] - diff[:, :-1]
    limited = 0.5 * limiter(curve[:, :-1], curve[:, 1:])
    inner = diff[:, 1 : n + 2]
    return inner[:, :n] + limited[:, :n], inner[:, 1:] - limited[:, 1:]


def lane_parts(here):
    axis, extent = here.ndim - 1, here.shape[-1]
    lanes = lax.broadcasted_iota(jnp.int32, here.shape, axis)
    low1, low2 = pltpu.roll(here, 1, axis), pltpu.roll(here, 2, axis)
    up1, up2 = pltpu.roll(here, extent - 1, axis), pltpu.roll(here, extent - 2, axis)
    below, above = here - low1, up1 - here
    diff1 = jnp.where(lanes == 0, above, below)
    diff2 = jnp.where(lanes == extent - 1, below, above)
    diff0 = jnp.where(lanes <= 1, diff1, low1 - low2)
    diff3 = jnp.where(lanes >= extent - 2, diff2, up2 - up1)
    return parts(diff0, diff1, diff2, diff3)


def heading_term(here, other):
    axis = here.ndim - 2
    rows = lax.broadcasted_iota(jnp.int32, here.shape, axis)
    low2 = pltpu.roll(jnp.where(rows >= 6, other, here), 2, axis)
    low1 = pltpu.roll(jnp.where(rows == 7, other, here), 1, axis)
    up1 = pltpu.roll(jnp.where(rows == 0, other, here), 7, axis)
    up2 = pltpu.roll(jnp.where(rows <= 1, other, here), 6, axis)
    backward, forward = parts(low1 - low2, here - low1, up1 - here, up2 - up1)
    return jnp.maximum(backward, -forward)


def speed_terms(values):
    diff = [values[i + 1] - values[i] for i in range(3)]
    limited = 0.5 * limiter(diff[1] - diff[0], diff[2] - diff[1])
    return jnp.stack([
        jnp.abs(diff[0]),
        jnp.maximum(diff[0], limited - diff[1]),
        jnp.maximum(diff[1] + limited, -diff[2]),
        jnp.abs(diff[2]),
    ])


def kernel(
    n_gx, n_ha, field_hbm, wind_hbm, obstacle_hbm, out_v,
    v_a, w_a, v_b, w_b, sec_t, sec_w, known, jump_x, jump_y, wind_int, wind_f, obst, peaks, drift,
    send_sem, recv_sem, wind_send, wind_recv, ready, local_sem,
):
    gx, ha = lax.axis_index("gx"), lax.axis_index("ha")
    head_step = 2.0 * math.pi / (8 * n_ha)

    loads = [
        pltpu.make_async_copy(wind_hbm, wind_int.at[:, :, 2:6], local_sem.at[0]),
        pltpu.make_async_copy(field_hbm.at[:, :, 0:4], v_a.at[:, 4:8, 4:8], local_sem.at[1]),
        pltpu.make_async_copy(field_hbm.at[:, :, 4:8], w_a.at[:, 2:6, 0:4], local_sem.at[2]),
        pltpu.make_async_copy(obstacle_hbm, obst, local_sem.at[3]),
    ]
    for copy in loads:
        copy.start()

    def has(dx):
        return (gx + dx >= 0) & (gx + dx < n_gx)

    below, above = lax.rem(ha + n_ha - 1, n_ha), lax.rem(ha + 1, n_ha)
    barrier = pltpu.get_barrier_semaphore()

    def signal(semaphore, x, h):
        pl.semaphore_signal(semaphore, inc=1, device_id=(x, h), device_id_type=MESH)

    signal(barrier, gx, below)
    for dx in (1, -1):
        pl.when(has(dx))(functools.partial(signal, barrier, gx + dx, below))

    @pl.loop(gx + 1, n_gx)
    def _(k):
        signal(barrier, k, ha)

    loads[1].wait()
    loads[2].wait()
    pl.semaphore_wait(
        barrier, 1 + gx + has(1).astype(jnp.int32) + has(-1).astype(jnp.int32)
    )

    def remote(src, dst, index, dx, dh):
        return pltpu.make_async_remote_copy(
            src_ref=src, dst_ref=dst, send_sem=send_sem.at[index], recv_sem=recv_sem.at[index],
            device_id=(gx + dx, lax.rem(ha + dh + n_ha, n_ha)), device_id_type=MESH,
        )

    def halo(v, w, base, way):
        low, high = slice(0, 4), slice(4, 8)
        mine, theirs = (high, low) if way > 0 else (low, high)
        inner, outer = (slice(0, 2), slice(6, 8)) if way > 0 else (slice(6, 8), slice(0, 2))

        copies, sides = [], ((1, slice(0, 4), slice(6, 8), slice(0, 2)), (-1, slice(8, 12), slice(4, 6), slice(6, 8)))
        for dx, to, near, far in sides:
            near_w = slice(near.start - 2, near.stop - 2)
            copies += [
                (dx, v.at[:, near, outer], w.at[:, far, outer], way),
                (dx, w.at[:, 2:6, theirs], v.at[:, to, theirs], way),
                (dx, w.at[:, near_w, inner], w.at[:, far, inner], 0),
                (dx, v.at[:, 4:8, mine], v.at[:, to, mine], 0),
            ]
        copies = [copies[n] for n in (0, 4, 1, 5)] + [
            (0, w.at[:, 2:6, theirs], v.at[:, 4:8, theirs], way),
            (0, v.at[:, 4:8, mine], w.at[:, 2:6, mine], way),
        ] + [copies[n] for n in (2, 6, 3, 7)]
        made = [
            (dx, remote(src, dst, base + n, dx, dh)) for n, (dx, src, dst, dh) in enumerate(copies)
        ]
        relays = [
            (-1, remote(w.at[:, 2:4, outer], w.at[:, 6:8, outer], base + 1, -1, 0)),
            (-1, remote(v.at[:, 4:8, theirs], v.at[:, 8:12, theirs], base + 3, -1, 0)),
        ]
        return made, relays

    odd = lax.rem(gx, 2) == 1

    def depart(copies):
        @pl.when(has(-1) & jnp.logical_not(odd))
        def _():
            copies[1][1].start()
            copies[3][1].start()

        start([copies[0], copies[2]] + copies[4:6])

    def relay(copies):
        @pl.when(odd)
        def _():
            for _, copy in copies:
                copy.start()

    def start(copies):
        for dx in (0, 1, -1):
            mine = [copy for d, copy in copies if d == dx]

            def run(mine=mine):
                for copy in mine:
                    copy.start()

            guarded(dx, mine, run)

    def receive(copies):
        for dx in (0, 1, -1):
            mine = [copy for d, copy in copies if d == dx]

            def run(mine=mine):
                for copy in mine:
                    copy.wait_recv()

            guarded(-dx, mine, run)

    def finish_sends(copies):
        for dx in (0, 1, -1):
            mine = [copy for d, copy in copies if d == dx]

            def run(mine=mine):
                for copy in mine:
                    copy.wait_send()

            guarded(dx, mine, run)

    def guarded(dx, mine, run):
        if not mine:
            return
        if dx == 0:
            run()
        else:
            pl.when(has(dx))(run)

    first, first_relays = halo(v_a, w_a, 0, 1)
    second, second_relays = halo(v_b, w_b, 10, -1)
    wind_edges = [
        (1, remote(wind_int.at[:, :, 4:6], wind_int.at[:, :, 0:2], 20, 1, 0)),
        (-1, remote(wind_int.at[:, :, 2:4], wind_int.at[:, :, 6:8], 21, -1, 0)),
    ]
    def wind_copy(k):
        return pltpu.make_async_remote_copy(
            src_ref=peaks.at[gx], dst_ref=peaks.at[gx], send_sem=wind_send, recv_sem=wind_recv,
            device_id=(k, ha), device_id_type=MESH,
        )

    line = pltpu.make_async_remote_copy(
        src_ref=peaks.at[0 : n_gx - 1], dst_ref=peaks.at[0 : n_gx - 1], send_sem=wind_send, recv_sem=wind_recv,
        device_id=(gx, above), device_id_type=MESH,
    )

    upward = [copy for n, copy in enumerate(first) if n in (6, 8)] + wind_edges[:1]
    depart(first)
    pl.when(has(-1))(lambda: signal(ready.at[0], gx - 1, ha))
    start([copy for n, copy in enumerate(first) if n in (7, 9)])

    @pl.loop(0, gx)
    def _(k):
        signal(ready.at[1], k, ha)

    loads[0].wait()
    quarters = lax.broadcasted_iota(jnp.int32, (1, 128), 1) // 32
    packed = jnp.zeros((1, 128), F32)
    for step in range(STEPS):
        for part in range(2):
            mine = jnp.max(jnp.abs(wind_int[step, part, 2:6, :].astype(F32) * WIND_SCALE), axis=0, keepdims=True)
            mine = jnp.max(mine, axis=1, keepdims=True)
            packed = jnp.where(quarters == 2 * step + part, mine, packed)
    peaks[gx] = packed
    start(wind_edges[1:])

    @pl.loop(0, gx)
    def _(k):
        wind_copy(k).start()

    half_scale = ACCEL_MAX / SPEED_STEP * 2.0
    head_scale = 2.0 * TURN_RATE / head_step
    own = slice(4, 8)

    def ends(ref, low, count, sides=(0, 1)):
        both = (
            (gx == 0, low, low + 1, low - 1, low - 2),
            (gx == n_gx - 1, low + count - 1, low + count - 2, low + count, low + count + 1),
        )
        for at_end, edge, next_one, near, far in [both[side] for side in sides]:
            a, b = ref[:, edge], ref[:, next_one]
            ref[:, near] = jnp.where(at_end, 2.0 * a - b, ref[:, near])
            ref[:, far] = jnp.where(at_end, 3.0 * a - 2.0 * b, ref[:, far])

    def across(step, tile, planes, here):
        back, fore = lane_parts(here)
        velocity = drift[step, tile, 1][:, None] + wind_f[step, 1, planes][None]
        return (back + fore) * velocity, fore - back

    def along(step, tile, planes, around):
        back, fore = plane_parts(around)
        velocity = drift[step, tile, 0][:, None] + wind_f[step, 0, planes][None]
        return (back + fore) * velocity, fore - back

    def begin(step, v, plane, count):
        place = pl.ds(plane - 2, count)
        values = v[:, pl.ds(plane, count)]
        mean, jump = across(step, 0, place, values)
        known[:, place] = mean - half_scale * speed_terms(values)
        jump_y[:, place] = jump

    def extend_x(step, v, block):
        place = pl.ds(block, 4)
        mean, jump = along(step, 0, place, v[:, pl.ds(block, 8)])
        known[:, place] = known[:, place] + mean
        jump_x[:, place] = jump

    def whole(step, tile, planes, around, here, other):
        alpha_x, alpha_y = alphas[step]
        mean_x, jump_at_x = along(step, tile, planes, around)
        mean_y, jump_at_y = across(step, tile, planes, here)
        result = mean_x + mean_y + alpha_x * jump_at_x + alpha_y * jump_at_y
        return halves[step] * (
            result - head_scale * heading_term(here, other) - half_scale * speed_terms(here)
        )

    def first_stage(step, v, w, block):
        alpha_x, alpha_y = alphas[step]
        place = pl.ds(block, 4)
        here, other = v[:, pl.ds(block + 2, 4)], w[:, place]
        rest = known[:, place] + alpha_x * jump_x[:, place] + alpha_y * jump_y[:, place]
        sec_t[:, place] = here + halves[step] * (rest - head_scale * heading_term(here, other))

    def wings(step, v, w, plane, count):
        planes = pl.ds(plane, count)
        here, beside = w[:, planes], v[:, pl.ds(plane + 2, count)]
        change = whole(step, 1, planes, w[:, pl.ds(plane - 2, count + 4)], here, beside)
        sec_w[:, pl.ds(plane - 2, count)] = here + change

    def second_stage(step, v, finish):
        ends(sec_t, 2, 4)
        here = sec_t[:, 2:6]
        change = whole(step, 0, pl.ds(2, 4), sec_t[...], here, sec_w[...])
        finish(0.5 * (v[:, own] + (here + change)))

    def limit(candidate, plane):
        blocked = jnp.broadcast_to(obst[pl.ds(plane, 1), :], (8, 128)) == 1
        value = candidate[:, plane]
        return jnp.where(blocked[None], jnp.maximum(value, OBSTACLE_LEVEL), value)

    def keep(candidate):
        for plane in range(4):
            swapped = pltpu.roll(limit(candidate, plane), 4, 1)
            v_b[:, 4 + plane, 0:4] = swapped[:, 0:4]
            w_b[:, 2 + plane, 4:8] = swapped[:, 4:8]
        start(second[6:])
        depart(second)

    def give(candidate):
        for plane in range(4):
            out_v[:, plane] = limit(candidate, plane)

    def spread(planes):
        for step in range(STEPS):
            for part in range(2):
                for plane in planes:
                    row = wind_int[step, part, pl.ds(plane, 1), :].astype(F32) * WIND_SCALE
                    wind_f[step, part, plane] = jnp.broadcast_to(row, (8, 128))

    spread(range(2, 6))
    rows = lax.broadcasted_iota(jnp.int32, (8, 128), 0)
    total = 8 * n_ha
    for tile in range(2):
        place = rows if tile == 0 else jnp.where(rows < 4, rows + 8, rows - 8)
        for step in range(STEPS):
            angle = lax.rem(ha * 8 + place + (total - 4 + 4 * step), total).astype(F32) * head_step
            for part, value in enumerate((jnp.cos(angle), jnp.sin(angle))):
                for s in range(4):
                    drift[step, tile, part, s] = (SPEED_BASE + SPEED_STEP * s) * value


    @pl.when(has(1))
    def _():
        pl.semaphore_wait(ready.at[0], 1)

    start(upward)

    @pl.when(gx < n_gx - 1)
    def _():
        pl.semaphore_wait(ready.at[1], n_gx - 1 - gx)

    @pl.loop(gx + 1, n_gx)
    def _(k):
        wind_copy(k).start()

    receive(wind_edges)
    spread((0, 1, 6, 7))

    loads[3].wait()
    receive(first[4:6])
    relay(first_relays)
    begin(0, v_a, 4, 4)
    line.wait_recv()
    receive([pair for pair in first[:4] + first[6:] if pair[0] == 1])

    highest = jnp.max(peaks[...], axis=0)
    quarters = lax.broadcasted_iota(jnp.int32, (1, 128), 1) // 32
    highest = [jnp.max(jnp.where(quarters == n, highest, 0.0), axis=1, keepdims=True) for n in range(4)]
    alphas, halves = [], []
    for step in range(STEPS):
        pair = [
            jnp.broadcast_to(SPEED_MAX + highest[2 * step + part], (8, 128))
            for part in range(2)
        ]
        alphas.append(pair)
        halves.append(
            (0.5 * CFL_NUMBER)
            / (pair[0] + pair[1] + (TURN_RATE / head_step + ACCEL_MAX / SPEED_STEP))
        )

    ends(v_a, 4, 4, (0,))
    ends(w_a, 2, 4, (0,))
    begin(0, v_a, 2, 2)
    extend_x(0, v_a, 0)
    first_stage(0, v_a, w_a, 0)
    wings(0, v_a, w_a, 2, 2)
    receive([pair for pair in first[:4] + first[6:] if pair[0] == -1])
    ends(v_a, 4, 4, (1,))
    ends(w_a, 2, 4, (1,))
    begin(0, v_a, 8, 2)
    extend_x(0, v_a, 4)
    first_stage(0, v_a, w_a, 4)
    wings(0, v_a, w_a, 4, 2)
    second_stage(0, v_a, keep)

    receive(second[4:6])
    relay(second_relays)
    begin(1, v_b, 4, 4)
    finish_sends(first + wind_edges)
    line.wait_send()

    parity = odd.astype(jnp.int32)
    near, far = 4 - 4 * parity, 4 * parity

    def side(copies, left):
        for copy in [copy for dx, copy in copies if dx == (1 if left else -1)]:
            copy.wait_recv()

    pl.when(odd)(functools.partial(side, second, True))
    pl.when(jnp.logical_not(odd))(functools.partial(side, second, False))
    begin(1, v_b, 2 + near + near // 2, 2)
    extend_x(1, v_b, near)
    first_stage(1, v_b, w_b, near)
    wings(1, v_b, w_b, 2 + near // 2, 2)
    finish_sends(second[6:])
    pl.when(odd & has(1))(functools.partial(side, second, False))
    pl.when(jnp.logical_not(odd) & has(-1))(functools.partial(side, second, True))
    ends(v_b, 4, 4)
    ends(w_b, 2, 4)
    begin(1, v_b, 2 + far + far // 2, 2)
    extend_x(1, v_b, far)
    first_stage(1, v_b, w_b, far)
    wings(1, v_b, w_b, 2 + far // 2, 2)
    second_stage(1, v_b, give)
    finish_sends(second[:6])


def solution(mesh):
    n_gx, n_ha = mesh.shape["gx"], mesh.shape["ha"]

    def local(value_field, wind_grid, obstacle):
        return pl.pallas_call(
            functools.partial(kernel, n_gx, n_ha),
            out_shape=jax.ShapeDtypeStruct(value_field.shape, F32),
            in_specs=[pl.BlockSpec(memory_space=pltpu.HBM)] * 3,
            out_specs=pl.BlockSpec(memory_space=pltpu.VMEM),
            scratch_shapes=[
                pltpu.VMEM((4, 12, 8, 128), F32),
                pltpu.VMEM((4, 8, 8, 128), F32),
                pltpu.VMEM((4, 12, 8, 128), F32),
                pltpu.VMEM((4, 8, 8, 128), F32),
                pltpu.VMEM((4, 8, 8, 128), F32),
                pltpu.VMEM((4, 4, 8, 128), F32),
                pltpu.VMEM((4, 8, 8, 128), F32),
                pltpu.VMEM((4, 8, 8, 128), F32),
                pltpu.VMEM((4, 8, 8, 128), F32),
                pltpu.VMEM((2, 2, 8, 128), jnp.int32),
                pltpu.VMEM((2, 2, 8, 8, 128), F32),
                pltpu.VMEM((4, 128), jnp.int32),
                pltpu.VMEM((n_gx, 1, 128), F32),
                pltpu.VMEM((2, 2, 2, 4, 8, 128), F32),
                pltpu.SemaphoreType.DMA((22,)),
                pltpu.SemaphoreType.DMA((22,)),
                pltpu.SemaphoreType.DMA,
                pltpu.SemaphoreType.DMA,
                pltpu.SemaphoreType.REGULAR((2,)),
                pltpu.SemaphoreType.DMA((4,)),
            ],
            compiler_params=pltpu.CompilerParams(collective_id=0, has_side_effects=True, vmem_limit_bytes=8 * 1024 * 1024),
            name="reach",
        )(*[pltpu.with_memory_space_constraint(x, pltpu.HBM) for x in (value_field, wind_grid, obstacle)])

    placed = (P(None, "gx", "ha", None), P(None, None, "gx", None), P("gx", None))
    return jax.shard_map(
        local, mesh=mesh, in_specs=placed, out_specs=P(None, "gx", "ha", None), check_vma=False
    )
```

```python
import functools
import math

import jax
import jax.numpy as jnp
from jax import lax
from jax.experimental import pallas as pl
from jax.experimental.pallas import tpu as pltpu
from jax.sharding import PartitionSpec as P

MESH = pl.DeviceIdType.MESH
STEPS = 2
TURN_RATE = 0.25
ACCEL_MAX = 0.5
SPEED_BASE = 0.5
SPEED_STEP = 0.25
SPEED_MAX = 1.25
WIND_SCALE = 1.0 / 512.0
CFL_NUMBER = 0.8
OBSTACLE_LEVEL = 1.0
F32 = jnp.float32


def limiter(before, here):
    return jnp.maximum(jnp.minimum(before, jnp.maximum(here, 0.0)), jnp.minimum(here, 0.0))


def parts(diff0, diff1, diff2, diff3):
    curve = diff2 - diff1
    backward = diff1 + 0.5 * limiter(diff1 - diff0, curve)
    forward = diff2 - 0.5 * limiter(curve, diff3 - diff2)
    return backward, forward


def plane_parts(values):
    n = values.shape[1] - 4
    diff = values[:, 1:] - values[:, :-1]
    curve = diff[:, 1:] - diff[:, :-1]
    limited = 0.5 * limiter(curve[:, :-1], curve[:, 1:])
    inner = diff[:, 1 : n + 2]
    return inner[:, :n] + limited[:, :n], inner[:, 1:] - limited[:, 1:]


def lane_parts(here):
    axis, extent = here.ndim - 1, here.shape[-1]
    lanes = lax.broadcasted_iota(jnp.int32, here.shape, axis)
    low1, low2 = pltpu.roll(here, 1, axis), pltpu.roll(here, 2, axis)
    up1, up2 = pltpu.roll(here, extent - 1, axis), pltpu.roll(here, extent - 2, axis)
    below, above = here - low1, up1 - here
    diff1 = jnp.where(lanes == 0, above, below)
    diff2 = jnp.where(lanes == extent - 1, below, above)
    diff0 = jnp.where(lanes <= 1, diff1, low1 - low2)
    diff3 = jnp.where(lanes >= extent - 2, diff2, up2 - up1)
    return parts(diff0, diff1, diff2, diff3)


def heading_term(here, other):
    axis = here.ndim - 2
    rows = lax.broadcasted_iota(jnp.int32, here.shape, axis)
    low2 = pltpu.roll(jnp.where(rows >= 6, other, here), 2, axis)
    low1 = pltpu.roll(jnp.where(rows == 7, other, here), 1, axis)
    up1 = pltpu.roll(jnp.where(rows == 0, other, here), 7, axis)
    up2 = pltpu.roll(jnp.where(rows <= 1, other, here), 6, axis)
    backward, forward = parts(low1 - low2, here - low1, up1 - here, up2 - up1)
    return jnp.maximum(backward, -forward)


def speed_terms(values):
    diff = [values[i + 1] - values[i] for i in range(3)]
    limited = 0.5 * limiter(diff[1] - diff[0], diff[2] - diff[1])
    return jnp.stack([
        jnp.abs(diff[0]),
        jnp.maximum(diff[0], limited - diff[1]),
        jnp.maximum(diff[1] + limited, -diff[2]),
        jnp.abs(diff[2]),
    ])


def kernel(
    n_gx, n_ha, field_hbm, wind_hbm, obstacle_hbm, out_v,
    v_a, w_a, v_b, w_b, sec_t, sec_w, known, jump_x, jump_y, wind_int, wind_f, obst, peaks, drift,
    send_sem, recv_sem, wind_send, wind_recv, ready, local_sem,
):
    gx, ha = lax.axis_index("gx"), lax.axis_index("ha")
    head_step = 2.0 * math.pi / (8 * n_ha)

    loads = [
        pltpu.make_async_copy(wind_hbm, wind_int.at[:, :, 2:6], local_sem.at[0]),
        pltpu.make_async_copy(field_hbm.at[:, :, 0:4], v_a.at[:, 4:8, 4:8], local_sem.at[1]),
        pltpu.make_async_copy(field_hbm.at[:, :, 4:8], w_a.at[:, 2:6, 0:4], local_sem.at[2]),
        pltpu.make_async_copy(obstacle_hbm, obst, local_sem.at[3]),
    ]
    for copy in loads:
        copy.start()

    def has(dx):
        return (gx + dx >= 0) & (gx + dx < n_gx)

    below, above = lax.rem(ha + n_ha - 1, n_ha), lax.rem(ha + 1, n_ha)
    barrier = pltpu.get_barrier_semaphore()

    def signal(semaphore, x, h):
        pl.semaphore_signal(semaphore, inc=1, device_id=(x, h), device_id_type=MESH)

    signal(barrier, gx, below)
    for dx in (1, -1):
        pl.when(has(dx))(functools.partial(signal, barrier, gx + dx, below))

    quarter = n_gx // 4

    def rank(g):
        four = g // 4
        moved = (lax.rem(g, 4) == 2) & (four > 0)
        return jnp.where(moved, n_gx - quarter + four, g - jnp.maximum(g - 3, 0) // 4)

    def column(r):
        kept = jnp.where(r < 6, r, r + 1 + jnp.maximum(r - 6, 0) // 3)
        return jnp.where(r > n_gx - quarter, 4 * (r - n_gx + quarter) + 2, kept)

    mine = rank(gx)
    first_up, first_down = has(1) & (mine > rank(gx + 1)), has(-1) & (mine > rank(gx - 1))
    later_up, later_down = has(1) & (mine < rank(gx + 1)), has(-1) & (mine < rank(gx - 1))

    @pl.loop(mine + 1, n_gx)
    def _(r):
        signal(barrier, column(r), ha)

    loads[1].wait()
    loads[2].wait()
    pl.semaphore_wait(
        barrier, 1 + mine + has(1).astype(jnp.int32) + has(-1).astype(jnp.int32)
    )

    def remote(src, dst, index, dx, dh):
        return pltpu.make_async_remote_copy(
            src_ref=src, dst_ref=dst, send_sem=send_sem.at[index], recv_sem=recv_sem.at[index],
            device_id=(gx + dx, lax.rem(ha + dh + n_ha, n_ha)), device_id_type=MESH,
        )

    def halo(v, w, base, way):
        low, high = slice(0, 4), slice(4, 8)
        mine, theirs = (high, low) if way > 0 else (low, high)
        inner, outer = (slice(0, 2), slice(6, 8)) if way > 0 else (slice(6, 8), slice(0, 2))

        copies, sides = [], ((1, slice(0, 4), slice(6, 8), slice(0, 2)), (-1, slice(8, 12), slice(4, 6), slice(6, 8)))
        for dx, to, near, far in sides:
            near_w = slice(near.start - 2, near.stop - 2)
            copies += [
                (dx, v.at[:, near, outer], w.at[:, far, outer], way),
                (dx, w.at[:, 2:6, theirs], v.at[:, to, theirs], way),
                (dx, w.at[:, near_w, inner], w.at[:, far, inner], 0),
                (dx, v.at[:, 4:8, mine], v.at[:, to, mine], 0),
            ]
        copies = [copies[n] for n in (0, 4, 1, 5)] + [
            (0, w.at[:, 2:6, theirs], v.at[:, 4:8, theirs], way),
            (0, v.at[:, 4:8, mine], w.at[:, 2:6, mine], way),
        ] + [copies[n] for n in (2, 6, 3, 7)]
        made = [
            (dx, remote(src, dst, base + n, dx, dh)) for n, (dx, src, dst, dh) in enumerate(copies)
        ]
        relays = [
            (-1, remote(w.at[:, 2:4, outer], w.at[:, 6:8, outer], base + 1, -1, 0)),
            (-1, remote(v.at[:, 4:8, theirs], v.at[:, 8:12, theirs], base + 3, -1, 0)),
        ]
        return made, relays

    odd = lax.rem(gx, 2) == 1

    def depart(copies):
        @pl.when(has(-1) & jnp.logical_not(odd))
        def _():
            copies[1][1].start()
            copies[3][1].start()

        start([copies[0], copies[2]] + copies[4:6])

    def relay(copies):
        @pl.when(odd)
        def _():
            for _, copy in copies:
                copy.start()

    def start(copies):
        for dx in (0, 1, -1):
            mine = [copy for d, copy in copies if d == dx]

            def run(mine=mine):
                for copy in mine:
                    copy.start()

            guarded(dx, mine, run)

    def receive(copies):
        for dx in (0, 1, -1):
            mine = [copy for d, copy in copies if d == dx]

            def run(mine=mine):
                for copy in mine:
                    copy.wait_recv()

            guarded(-dx, mine, run)

    def finish_sends(copies):
        for dx in (0, 1, -1):
            mine = [copy for d, copy in copies if d == dx]

            def run(mine=mine):
                for copy in mine:
                    copy.wait_send()

            guarded(dx, mine, run)

    def guarded(dx, mine, run):
        if not mine:
            return
        if dx == 0:
            run()
        else:
            pl.when(has(dx))(run)

    first, first_relays = halo(v_a, w_a, 0, 1)
    second, second_relays = halo(v_b, w_b, 10, -1)
    wind_edges = [
        (1, remote(wind_int.at[:, :, 4:6], wind_int.at[:, :, 0:2], 20, 1, 0)),
        (-1, remote(wind_int.at[:, :, 2:4], wind_int.at[:, :, 6:8], 21, -1, 0)),
    ]
    def wind_copy(k):
        return pltpu.make_async_remote_copy(
            src_ref=peaks.at[gx], dst_ref=peaks.at[gx], send_sem=wind_send, recv_sem=wind_recv,
            device_id=(k, ha), device_id_type=MESH,
        )

    line = pltpu.make_async_remote_copy(
        src_ref=peaks.at[0 : n_gx - 1], dst_ref=peaks.at[0 : n_gx - 1], send_sem=wind_send, recv_sem=wind_recv,
        device_id=(gx, above), device_id_type=MESH,
    )

    upward = [copy for n, (_, copy) in enumerate(first) if n in (6, 8)] + [wind_edges[0][1]]
    downward = [copy for n, (_, copy) in enumerate(first) if n in (7, 9)] + [wind_edges[1][1]]
    depart(first)

    @pl.when(first_up)
    def _():
        signal(ready.at[0], gx + 1, ha)

    @pl.when(first_down)
    def _():
        signal(ready.at[0], gx - 1, ha)

    loads[0].wait()

    def begin_x(up, down):
        for condition, copies in ((up, upward), (down, downward)):

            @pl.when(condition)
            def _(copies=copies):
                for copy in copies:
                    copy.start()

    begin_x(first_up, first_down)

    @pl.loop(0, mine)
    def _(r):
        signal(ready.at[1], column(r), ha)

    quarters = lax.broadcasted_iota(jnp.int32, (1, 128), 1) // 32
    packed = jnp.zeros((1, 128), F32)
    for step in range(STEPS):
        for part in range(2):
            largest = jnp.max(jnp.abs(wind_int[step, part, 2:6, :].astype(F32) * WIND_SCALE), axis=0, keepdims=True)
            largest = jnp.max(largest, axis=1, keepdims=True)
            packed = jnp.where(quarters == 2 * step + part, largest, packed)
    peaks[gx] = packed

    @pl.loop(0, mine)
    def _(r):
        wind_copy(column(r)).start()

    half_scale = ACCEL_MAX / SPEED_STEP * 2.0
    head_scale = 2.0 * TURN_RATE / head_step
    own = slice(4, 8)

    def ends(ref, low, count, sides=(0, 1)):
        both = (
            (gx == 0, low, low + 1, low - 1, low - 2),
            (gx == n_gx - 1, low + count - 1, low + count - 2, low + count, low + count + 1),
        )
        for at_end, edge, next_one, near, far in [both[side] for side in sides]:
            a, b = ref[:, edge], ref[:, next_one]
            ref[:, near] = jnp.where(at_end, 2.0 * a - b, ref[:, near])
            ref[:, far] = jnp.where(at_end, 3.0 * a - 2.0 * b, ref[:, far])

    def across(step, tile, planes, here):
        back, fore = lane_parts(here)
        velocity = drift[step, tile, 1][:, None] + wind_f[step, 1, planes][None]
        return (back + fore) * velocity, fore - back

    def along(step, tile, planes, around):
        back, fore = plane_parts(around)
        velocity = drift[step, tile, 0][:, None] + wind_f[step, 0, planes][None]
        return (back + fore) * velocity, fore - back

    def begin(step, v, plane, count):
        place = pl.ds(plane - 2, count)
        values = v[:, pl.ds(plane, count)]
        mean, jump = across(step, 0, place, values)
        known[:, place] = mean - half_scale * speed_terms(values)
        jump_y[:, place] = jump

    def extend_x(step, v, block):
        place = pl.ds(block, 4)
        mean, jump = along(step, 0, place, v[:, pl.ds(block, 8)])
        known[:, place] = known[:, place] + mean
        jump_x[:, place] = jump

    def whole(step, tile, planes, around, here, other):
        alpha_x, alpha_y = alphas[step]
        mean_x, jump_at_x = along(step, tile, planes, around)
        mean_y, jump_at_y = across(step, tile, planes, here)
        result = mean_x + mean_y + alpha_x * jump_at_x + alpha_y * jump_at_y
        return halves[step] * (
            result - head_scale * heading_term(here, other) - half_scale * speed_terms(here)
        )

    def first_stage(step, v, w, block):
        alpha_x, alpha_y = alphas[step]
        place = pl.ds(block, 4)
        here, other = v[:, pl.ds(block + 2, 4)], w[:, place]
        rest = known[:, place] + alpha_x * jump_x[:, place] + alpha_y * jump_y[:, place]
        sec_t[:, place] = here + halves[step] * (rest - head_scale * heading_term(here, other))

    def wings(step, v, w, plane, count):
        planes = pl.ds(plane, count)
        here, beside = w[:, planes], v[:, pl.ds(plane + 2, count)]
        change = whole(step, 1, planes, w[:, pl.ds(plane - 2, count + 4)], here, beside)
        sec_w[:, pl.ds(plane - 2, count)] = here + change

    def second_stage(step, v, finish):
        ends(sec_t, 2, 4)
        here = sec_t[:, 2:6]
        change = whole(step, 0, pl.ds(2, 4), sec_t[...], here, sec_w[...])
        finish(0.5 * (v[:, own] + (here + change)))

    def limit(candidate, plane):
        blocked = jnp.broadcast_to(obst[pl.ds(plane, 1), :], (8, 128)) == 1
        value = candidate[:, plane]
        return jnp.where(blocked[None], jnp.maximum(value, OBSTACLE_LEVEL), value)

    def keep(candidate):
        for plane in range(4):
            swapped = pltpu.roll(limit(candidate, plane), 4, 1)
            v_b[:, 4 + plane, 0:4] = swapped[:, 0:4]
            w_b[:, 2 + plane, 4:8] = swapped[:, 4:8]
        start(second[6:])
        depart(second)

    def give(candidate):
        for plane in range(4):
            out_v[:, plane] = limit(candidate, plane)

    def spread(planes):
        for step in range(STEPS):
            for part in range(2):
                for plane in planes:
                    row = wind_int[step, part, pl.ds(plane, 1), :].astype(F32) * WIND_SCALE
                    wind_f[step, part, plane] = jnp.broadcast_to(row, (8, 128))

    spread(range(2, 6))
    rows = lax.broadcasted_iota(jnp.int32, (8, 128), 0)
    total = 8 * n_ha
    for tile in range(2):
        place = rows if tile == 0 else jnp.where(rows < 4, rows + 8, rows - 8)
        for step in range(STEPS):
            angle = lax.rem(ha * 8 + place + (total - 4 + 4 * step), total).astype(F32) * head_step
            for part, value in enumerate((jnp.cos(angle), jnp.sin(angle))):
                for s in range(4):
                    drift[step, tile, part, s] = (SPEED_BASE + SPEED_STEP * s) * value


    @pl.when(later_up | later_down)
    def _():
        pl.semaphore_wait(ready.at[0], later_up.astype(jnp.int32) + later_down.astype(jnp.int32))

    begin_x(later_up, later_down)

    @pl.when(mine < n_gx - 1)
    def _():
        pl.semaphore_wait(ready.at[1], n_gx - 1 - mine)

    @pl.loop(mine + 1, n_gx)
    def _(r):
        wind_copy(column(r)).start()

    receive(wind_edges)
    spread((0, 1, 6, 7))

    loads[3].wait()
    receive(first[4:6])
    relay(first_relays)
    begin(0, v_a, 4, 4)
    line.wait_recv()
    receive([pair for pair in first[:4] + first[6:] if pair[0] == 1])

    highest = jnp.max(peaks[...], axis=0)
    quarters = lax.broadcasted_iota(jnp.int32, (1, 128), 1) // 32
    highest = [jnp.max(jnp.where(quarters == n, highest, 0.0), axis=1, keepdims=True) for n in range(4)]
    alphas, halves = [], []
    for step in range(STEPS):
        pair = [
            jnp.broadcast_to(SPEED_MAX + highest[2 * step + part], (8, 128))
            for part in range(2)
        ]
        alphas.append(pair)
        halves.append(
            (0.5 * CFL_NUMBER)
            / (pair[0] + pair[1] + (TURN_RATE / head_step + ACCEL_MAX / SPEED_STEP))
        )

    ends(v_a, 4, 4, (0,))
    ends(w_a, 2, 4, (0,))
    begin(0, v_a, 2, 2)
    extend_x(0, v_a, 0)
    first_stage(0, v_a, w_a, 0)
    wings(0, v_a, w_a, 2, 2)
    receive([pair for pair in first[:4] + first[6:] if pair[0] == -1])
    ends(v_a, 4, 4, (1,))
    ends(w_a, 2, 4, (1,))
    begin(0, v_a, 8, 2)
    extend_x(0, v_a, 4)
    first_stage(0, v_a, w_a, 4)
    wings(0, v_a, w_a, 4, 2)
    second_stage(0, v_a, keep)

    receive(second[4:6])
    relay(second_relays)
    begin(1, v_b, 4, 4)
    finish_sends(first + wind_edges)
    line.wait_send()

    parity = odd.astype(jnp.int32)
    near, far = 4 - 4 * parity, 4 * parity

    def side(copies, left):
        for copy in [copy for dx, copy in copies if dx == (1 if left else -1)]:
            copy.wait_recv()

    pl.when(odd)(functools.partial(side, second, True))
    pl.when(jnp.logical_not(odd))(functools.partial(side, second, False))
    begin(1, v_b, 2 + near + near // 2, 2)
    extend_x(1, v_b, near)
    first_stage(1, v_b, w_b, near)
    wings(1, v_b, w_b, 2 + near // 2, 2)
    finish_sends(second[6:])
    pl.when(odd & has(1))(functools.partial(side, second, False))
    pl.when(jnp.logical_not(odd) & has(-1))(functools.partial(side, second, True))
    ends(v_b, 4, 4)
    ends(w_b, 2, 4)
    begin(1, v_b, 2 + far + far // 2, 2)
    extend_x(1, v_b, far)
    first_stage(1, v_b, w_b, far)
    wings(1, v_b, w_b, 2 + far // 2, 2)
    second_stage(1, v_b, give)
    finish_sends(second[:6])


def solution(mesh):
    n_gx, n_ha = mesh.shape["gx"], mesh.shape["ha"]

    def local(value_field, wind_grid, obstacle):
        return pl.pallas_call(
            functools.partial(kernel, n_gx, n_ha),
            out_shape=jax.ShapeDtypeStruct(value_field.shape, F32),
            in_specs=[pl.BlockSpec(memory_space=pltpu.HBM)] * 3,
            out_specs=pl.BlockSpec(memory_space=pltpu.VMEM),
            scratch_shapes=[
                pltpu.VMEM((4, 12, 8, 128), F32),
                pltpu.VMEM((4, 8, 8, 128), F32),
                pltpu.VMEM((4, 12, 8, 128), F32),
                pltpu.VMEM((4, 8, 8, 128), F32),
                pltpu.VMEM((4, 8, 8, 128), F32),
                pltpu.VMEM((4, 4, 8, 128), F32),
                pltpu.VMEM((4, 8, 8, 128), F32),
                pltpu.VMEM((4, 8, 8, 128), F32),
                pltpu.VMEM((4, 8, 8, 128), F32),
                pltpu.VMEM((2, 2, 8, 128), jnp.int32),
                pltpu.VMEM((2, 2, 8, 8, 128), F32),
                pltpu.VMEM((4, 128), jnp.int32),
                pltpu.VMEM((n_gx, 1, 128), F32),
                pltpu.VMEM((2, 2, 2, 4, 8, 128), F32),
                pltpu.SemaphoreType.DMA((22,)),
                pltpu.SemaphoreType.DMA((22,)),
                pltpu.SemaphoreType.DMA,
                pltpu.SemaphoreType.DMA,
                pltpu.SemaphoreType.REGULAR((2,)),
                pltpu.SemaphoreType.DMA((4,)),
            ],
            compiler_params=pltpu.CompilerParams(collective_id=0, has_side_effects=True, vmem_limit_bytes=8 * 1024 * 1024),
            name="reach",
        )(*[pltpu.with_memory_space_constraint(x, pltpu.HBM) for x in (value_field, wind_grid, obstacle)])

    placed = (P(None, "gx", "ha", None), P(None, None, "gx", None), P("gx", None))
    return jax.shard_map(
        local, mesh=mesh, in_specs=placed, out_specs=P(None, "gx", "ha", None), check_vma=False
    )
```

```python
import functools
import math

import jax
import jax.numpy as jnp
from jax import lax
from jax.experimental import pallas as pl
from jax.experimental.pallas import tpu as pltpu
from jax.sharding import PartitionSpec as P

MESH = pl.DeviceIdType.MESH
STEPS = 2
TURN_RATE = 0.25
ACCEL_MAX = 0.5
SPEED_BASE = 0.5
SPEED_STEP = 0.25
SPEED_MAX = 1.25
WIND_SCALE = 1.0 / 512.0
CFL_NUMBER = 0.8
OBSTACLE_LEVEL = 1.0
F32 = jnp.float32


def limiter(before, here):
    return jnp.maximum(jnp.minimum(before, jnp.maximum(here, 0.0)), jnp.minimum(here, 0.0))


def parts(diff0, diff1, diff2, diff3):
    curve = diff2 - diff1
    backward = diff1 + 0.5 * limiter(diff1 - diff0, curve)
    forward = diff2 - 0.5 * limiter(curve, diff3 - diff2)
    return backward, forward


def plane_parts(values):
    n = values.shape[1] - 4
    diff = values[:, 1:] - values[:, :-1]
    curve = diff[:, 1:] - diff[:, :-1]
    limited = 0.5 * limiter(curve[:, :-1], curve[:, 1:])
    inner = diff[:, 1 : n + 2]
    return inner[:, :n] + limited[:, :n], inner[:, 1:] - limited[:, 1:]


def lane_parts(here):
    axis, extent = here.ndim - 1, here.shape[-1]
    lanes = lax.broadcasted_iota(jnp.int32, here.shape, axis)
    low1, low2 = pltpu.roll(here, 1, axis), pltpu.roll(here, 2, axis)
    up1, up2 = pltpu.roll(here, extent - 1, axis), pltpu.roll(here, extent - 2, axis)
    below, above = here - low1, up1 - here
    diff1 = jnp.where(lanes == 0, above, below)
    diff2 = jnp.where(lanes == extent - 1, below, above)
    diff0 = jnp.where(lanes <= 1, diff1, low1 - low2)
    diff3 = jnp.where(lanes >= extent - 2, diff2, up2 - up1)
    return parts(diff0, diff1, diff2, diff3)


def heading_term(here, other):
    axis = here.ndim - 2
    rows = lax.broadcasted_iota(jnp.int32, here.shape, axis)
    low2 = pltpu.roll(jnp.where(rows >= 6, other, here), 2, axis)
    low1 = pltpu.roll(jnp.where(rows == 7, other, here), 1, axis)
    up1 = pltpu.roll(jnp.where(rows == 0, other, here), 7, axis)
    up2 = pltpu.roll(jnp.where(rows <= 1, other, here), 6, axis)
    backward, forward = parts(low1 - low2, here - low1, up1 - here, up2 - up1)
    return jnp.maximum(backward, -forward)


def speed_terms(values):
    diff = [values[i + 1] - values[i] for i in range(3)]
    limited = 0.5 * limiter(diff[1] - diff[0], diff[2] - diff[1])
    return jnp.stack([
        jnp.abs(diff[0]),
        jnp.maximum(diff[0], limited - diff[1]),
        jnp.maximum(diff[1] + limited, -diff[2]),
        jnp.abs(diff[2]),
    ])


def kernel(
    n_gx, n_ha, field_hbm, wind_hbm, obstacle_hbm, out_v,
    v_a, w_a, v_b, w_b, sec_t, sec_w, known, jump_x, jump_y, wind_int, wind_f, obst, peaks, drift,
    send_sem, recv_sem, wind_send, wind_recv, ready, local_sem,
):
    gx, ha = lax.axis_index("gx"), lax.axis_index("ha")
    head_step = 2.0 * math.pi / (8 * n_ha)

    loads = [
        pltpu.make_async_copy(wind_hbm, wind_int.at[:, :, 2:6], local_sem.at[0]),
        pltpu.make_async_copy(field_hbm.at[:, :, 0:4], v_a.at[:, 4:8, 4:8], local_sem.at[1]),
        pltpu.make_async_copy(field_hbm.at[:, :, 4:8], w_a.at[:, 2:6, 0:4], local_sem.at[2]),
        pltpu.make_async_copy(obstacle_hbm, obst, local_sem.at[3]),
    ]
    for copy in loads:
        copy.start()

    def has(dx):
        return (gx + dx >= 0) & (gx + dx < n_gx)

    below, above = lax.rem(ha + n_ha - 1, n_ha), lax.rem(ha + 1, n_ha)
    barrier = pltpu.get_barrier_semaphore()

    def signal(semaphore, x, h):
        pl.semaphore_signal(semaphore, inc=1, device_id=(x, h), device_id_type=MESH)

    signal(barrier, gx, below)
    for dx in (1, -1):
        pl.when(has(dx))(functools.partial(signal, barrier, gx + dx, below))

    quarter = n_gx // 4

    def rank(g):
        four = g // 4
        moved = (lax.rem(g, 4) == 2) & (four > 0)
        return jnp.where(moved, n_gx - quarter + four, g - jnp.maximum(g - 3, 0) // 4)

    def column(r):
        kept = jnp.where(r < 6, r, r + 1 + jnp.maximum(r - 6, 0) // 3)
        return jnp.where(r > n_gx - quarter, 4 * (r - n_gx + quarter) + 2, kept)

    mine = rank(gx)
    first_up, first_down = has(1) & (mine > rank(gx + 1)), has(-1) & (mine > rank(gx - 1))
    later_up, later_down = has(1) & (mine < rank(gx + 1)), has(-1) & (mine < rank(gx - 1))

    @pl.loop(mine + 1, n_gx)
    def _(r):
        signal(barrier, column(r), ha)

    loads[1].wait()
    loads[2].wait()
    pl.semaphore_wait(
        barrier, 1 + mine + has(1).astype(jnp.int32) + has(-1).astype(jnp.int32)
    )

    def remote(src, dst, index, dx, dh):
        return pltpu.make_async_remote_copy(
            src_ref=src, dst_ref=dst, send_sem=send_sem.at[index], recv_sem=recv_sem.at[index],
            device_id=(gx + dx, lax.rem(ha + dh + n_ha, n_ha)), device_id_type=MESH,
        )

    def halo(v, w, base, way):
        low, high = slice(0, 4), slice(4, 8)
        mine, theirs = (high, low) if way > 0 else (low, high)
        inner, outer = (slice(0, 2), slice(6, 8)) if way > 0 else (slice(6, 8), slice(0, 2))

        copies, sides = [], ((1, slice(0, 4), slice(6, 8), slice(0, 2)), (-1, slice(8, 12), slice(4, 6), slice(6, 8)))
        for dx, to, near, far in sides:
            near_w = slice(near.start - 2, near.stop - 2)
            copies += [
                (dx, v.at[:, near, outer], w.at[:, far, outer], way),
                (dx, w.at[:, 2:6, theirs], v.at[:, to, theirs], way),
                (dx, w.at[:, near_w, inner], w.at[:, far, inner], 0),
                (dx, v.at[:, 4:8, mine], v.at[:, to, mine], 0),
            ]
        copies = [copies[n] for n in (0, 4, 1, 5)] + [
            (0, w.at[:, 2:6, theirs], v.at[:, 4:8, theirs], way),
            (0, v.at[:, 4:8, mine], w.at[:, 2:6, mine], way),
        ] + [copies[n] for n in (2, 6, 3, 7)]
        made = [
            (dx, remote(src, dst, base + n, dx, dh)) for n, (dx, src, dst, dh) in enumerate(copies)
        ]
        relays = [
            (-1, remote(w.at[:, 2:4, outer], w.at[:, 6:8, outer], base + 1, -1, 0)),
            (-1, remote(v.at[:, 4:8, theirs], v.at[:, 8:12, theirs], base + 3, -1, 0)),
        ]
        return made, relays

    odd = lax.rem(gx, 2) == 1

    def depart(copies):
        @pl.when(has(-1) & jnp.logical_not(odd))
        def _():
            copies[1][1].start()
            copies[3][1].start()

        start([copies[0], copies[2]] + copies[4:6])

    def relay(copies):
        @pl.when(odd)
        def _():
            for _, copy in copies:
                copy.start()

    def start(copies):
        for dx in (0, 1, -1):
            mine = [copy for d, copy in copies if d == dx]

            def run(mine=mine):
                for copy in mine:
                    copy.start()

            guarded(dx, mine, run)

    def receive(copies):
        for dx in (0, 1, -1):
            mine = [copy for d, copy in copies if d == dx]

            def run(mine=mine):
                for copy in mine:
                    copy.wait_recv()

            guarded(-dx, mine, run)

    def finish_sends(copies):
        for dx in (0, 1, -1):
            mine = [copy for d, copy in copies if d == dx]

            def run(mine=mine):
                for copy in mine:
                    copy.wait_send()

            guarded(dx, mine, run)

    def guarded(dx, mine, run):
        if not mine:
            return
        if dx == 0:
            run()
        else:
            pl.when(has(dx))(run)

    first, first_relays = halo(v_a, w_a, 0, 1)
    second, second_relays = halo(v_b, w_b, 10, -1)
    wind_edges = [
        (1, remote(wind_int.at[:, :, 4:6], wind_int.at[:, :, 0:2], 20, 1, 0)),
        (-1, remote(wind_int.at[:, :, 2:4], wind_int.at[:, :, 6:8], 21, -1, 0)),
    ]
    def wind_copy(k):
        return pltpu.make_async_remote_copy(
            src_ref=peaks.at[gx], dst_ref=peaks.at[gx], send_sem=wind_send, recv_sem=wind_recv,
            device_id=(k, ha), device_id_type=MESH,
        )

    line = pltpu.make_async_remote_copy(
        src_ref=peaks.at[0 : n_gx - 1], dst_ref=peaks.at[0 : n_gx - 1], send_sem=wind_send, recv_sem=wind_recv,
        device_id=(gx, above), device_id_type=MESH,
    )

    upward = [copy for n, (_, copy) in enumerate(first) if n in (6, 8)] + [wind_edges[0][1]]
    downward = [copy for n, (_, copy) in enumerate(first) if n in (7, 9)] + [wind_edges[1][1]]
    depart(first)

    @pl.when(first_up)
    def _():
        signal(ready.at[0], gx + 1, ha)

    @pl.when(first_down)
    def _():
        signal(ready.at[0], gx - 1, ha)

    loads[0].wait()

    def begin_x(up, down):
        for condition, copies in ((up, upward), (down, downward)):

            @pl.when(condition)
            def _(copies=copies):
                for copy in copies:
                    copy.start()

    begin_x(first_up, first_down)

    @pl.loop(0, mine)
    def _(r):
        signal(ready.at[1], column(r), ha)

    quarters = lax.broadcasted_iota(jnp.int32, (1, 128), 1) // 32
    packed = jnp.zeros((1, 128), F32)
    for step in range(STEPS):
        for part in range(2):
            largest = jnp.max(jnp.abs(wind_int[step, part, 2:6, :].astype(F32) * WIND_SCALE), axis=0, keepdims=True)
            largest = jnp.max(largest, axis=1, keepdims=True)
            packed = jnp.where(quarters == 2 * step + part, largest, packed)
    peaks[gx] = packed

    @pl.loop(0, mine)
    def _(r):
        wind_copy(column(r)).start()

    half_scale = ACCEL_MAX / SPEED_STEP * 2.0
    head_scale = 2.0 * TURN_RATE / head_step
    own = slice(4, 8)

    def ends(ref, low, count, sides=(0, 1)):
        both = (
            (gx == 0, low, low + 1, low - 1, low - 2),
            (gx == n_gx - 1, low + count - 1, low + count - 2, low + count, low + count + 1),
        )
        for at_end, edge, next_one, near, far in [both[side] for side in sides]:
            a, b = ref[:, edge], ref[:, next_one]
            ref[:, near] = jnp.where(at_end, 2.0 * a - b, ref[:, near])
            ref[:, far] = jnp.where(at_end, 3.0 * a - 2.0 * b, ref[:, far])

    def across(step, tile, planes, here):
        back, fore = lane_parts(here)
        velocity = drift[step, tile, 1][:, None] + wind_f[step, 1, planes][None]
        return (back + fore) * velocity, fore - back

    def along(step, tile, planes, around):
        back, fore = plane_parts(around)
        velocity = drift[step, tile, 0][:, None] + wind_f[step, 0, planes][None]
        return (back + fore) * velocity, fore - back

    def begin(step, v, plane, count):
        place = pl.ds(plane - 2, count)
        values = v[:, pl.ds(plane, count)]
        mean, jump = across(step, 0, place, values)
        known[:, place] = mean - half_scale * speed_terms(values)
        jump_y[:, place] = jump

    def extend_x(step, v, block):
        place = pl.ds(block, 4)
        mean, jump = along(step, 0, place, v[:, pl.ds(block, 8)])
        known[:, place] = known[:, place] + mean
        jump_x[:, place] = jump

    def whole(step, tile, planes, around, here, other):
        alpha_x, alpha_y = alphas[step]
        mean_x, jump_at_x = along(step, tile, planes, around)
        mean_y, jump_at_y = across(step, tile, planes, here)
        result = mean_x + mean_y + alpha_x * jump_at_x + alpha_y * jump_at_y
        return halves[step] * (
            result - head_scale * heading_term(here, other) - half_scale * speed_terms(here)
        )

    def first_stage(step, v, w, block):
        alpha_x, alpha_y = alphas[step]
        place = pl.ds(block, 4)
        here, other = v[:, pl.ds(block + 2, 4)], w[:, place]
        rest = known[:, place] + alpha_x * jump_x[:, place] + alpha_y * jump_y[:, place]
        sec_t[:, place] = here + halves[step] * (rest - head_scale * heading_term(here, other))

    def wings(step, v, w, plane, count):
        planes = pl.ds(plane, count)
        here, beside = w[:, planes], v[:, pl.ds(plane + 2, count)]
        change = whole(step, 1, planes, w[:, pl.ds(plane - 2, count + 4)], here, beside)
        sec_w[:, pl.ds(plane - 2, count)] = here + change

    def second_stage(step, v, finish):
        ends(sec_t, 2, 4)
        here = sec_t[:, 2:6]
        change = whole(step, 0, pl.ds(2, 4), sec_t[...], here, sec_w[...])
        finish(0.5 * (v[:, own] + (here + change)))

    def limit(candidate, plane):
        blocked = jnp.broadcast_to(obst[pl.ds(plane, 1), :], (8, 128)) == 1
        value = candidate[:, plane]
        return jnp.where(blocked[None], jnp.maximum(value, OBSTACLE_LEVEL), value)

    def keep(candidate):
        for plane in range(4):
            swapped = pltpu.roll(limit(candidate, plane), 4, 1)
            v_b[:, 4 + plane, 0:4] = swapped[:, 0:4]
            w_b[:, 2 + plane, 4:8] = swapped[:, 4:8]
        start(second[6:])
        depart(second)

    def give(candidate):
        for plane in range(4):
            out_v[:, plane] = limit(candidate, plane)

    def spread(planes):
        for step in range(STEPS):
            for part in range(2):
                for plane in planes:
                    row = wind_int[step, part, pl.ds(plane, 1), :].astype(F32) * WIND_SCALE
                    wind_f[step, part, plane] = jnp.broadcast_to(row, (8, 128))

    spread(range(2, 6))
    rows = lax.broadcasted_iota(jnp.int32, (8, 128), 0)
    total = 8 * n_ha
    for tile in range(2):
        place = rows if tile == 0 else jnp.where(rows < 4, rows + 8, rows - 8)
        for step in range(STEPS):
            angle = lax.rem(ha * 8 + place + (total - 4 + 4 * step), total).astype(F32) * head_step
            for part, value in enumerate((jnp.cos(angle), jnp.sin(angle))):
                for s in range(4):
                    drift[step, tile, part, s] = (SPEED_BASE + SPEED_STEP * s) * value


    @pl.when(later_up | later_down)
    def _():
        pl.semaphore_wait(ready.at[0], later_up.astype(jnp.int32) + later_down.astype(jnp.int32))

    begin_x(later_up, later_down)

    @pl.when(mine < n_gx - 1)
    def _():
        pl.semaphore_wait(ready.at[1], n_gx - 1 - mine)

    @pl.loop(mine + 1, n_gx)
    def _(r):
        wind_copy(column(r)).start()

    receive(wind_edges)
    spread((0, 1, 6, 7))

    loads[3].wait()
    line.wait_recv()
    highest = jnp.max(peaks[...], axis=0)
    quarters = lax.broadcasted_iota(jnp.int32, (1, 128), 1) // 32
    highest = [jnp.max(jnp.where(quarters == n, highest, 0.0), axis=1, keepdims=True) for n in range(4)]
    alphas, halves = [], []
    for step in range(STEPS):
        pair = [
            jnp.broadcast_to(SPEED_MAX + highest[2 * step + part], (8, 128))
            for part in range(2)
        ]
        alphas.append(pair)
        halves.append(
            (0.5 * CFL_NUMBER)
            / (pair[0] + pair[1] + (TURN_RATE / head_step + ACCEL_MAX / SPEED_STEP))
        )

    receive(first[4:6])
    relay(first_relays)
    begin(0, v_a, 4, 4)
    receive([pair for pair in first[:4] + first[6:] if pair[0] == 1])

    ends(v_a, 4, 4, (0,))
    ends(w_a, 2, 4, (0,))
    begin(0, v_a, 2, 2)
    extend_x(0, v_a, 0)
    first_stage(0, v_a, w_a, 0)
    wings(0, v_a, w_a, 2, 2)
    receive([pair for pair in first[:4] + first[6:] if pair[0] == -1])
    ends(v_a, 4, 4, (1,))
    ends(w_a, 2, 4, (1,))
    begin(0, v_a, 8, 2)
    extend_x(0, v_a, 4)
    first_stage(0, v_a, w_a, 4)
    wings(0, v_a, w_a, 4, 2)
    second_stage(0, v_a, keep)

    receive(second[4:6])
    relay(second_relays)
    begin(1, v_b, 4, 4)
    finish_sends(first + wind_edges)
    line.wait_send()

    parity = odd.astype(jnp.int32)
    near, far = 4 - 4 * parity, 4 * parity

    def side(copies, left):
        for copy in [copy for dx, copy in copies if dx == (1 if left else -1)]:
            copy.wait_recv()

    pl.when(odd)(functools.partial(side, second, True))
    pl.when(jnp.logical_not(odd))(functools.partial(side, second, False))
    begin(1, v_b, 2 + near + near // 2, 2)
    extend_x(1, v_b, near)
    first_stage(1, v_b, w_b, near)
    wings(1, v_b, w_b, 2 + near // 2, 2)
    finish_sends(second[6:])
    pl.when(odd & has(1))(functools.partial(side, second, False))
    pl.when(jnp.logical_not(odd) & has(-1))(functools.partial(side, second, True))
    ends(v_b, 4, 4)
    ends(w_b, 2, 4)
    begin(1, v_b, 2 + far + far // 2, 2)
    extend_x(1, v_b, far)
    first_stage(1, v_b, w_b, far)
    wings(1, v_b, w_b, 2 + far // 2, 2)
    second_stage(1, v_b, give)
    finish_sends(second[:6])


def solution(mesh):
    n_gx, n_ha = mesh.shape["gx"], mesh.shape["ha"]

    def local(value_field, wind_grid, obstacle):
        return pl.pallas_call(
            functools.partial(kernel, n_gx, n_ha),
            out_shape=jax.ShapeDtypeStruct(value_field.shape, F32),
            in_specs=[pl.BlockSpec(memory_space=pltpu.HBM)] * 3,
            out_specs=pl.BlockSpec(memory_space=pltpu.VMEM),
            scratch_shapes=[
                pltpu.VMEM((4, 12, 8, 128), F32),
                pltpu.VMEM((4, 8, 8, 128), F32),
                pltpu.VMEM((4, 12, 8, 128), F32),
                pltpu.VMEM((4, 8, 8, 128), F32),
                pltpu.VMEM((4, 8, 8, 128), F32),
                pltpu.VMEM((4, 4, 8, 128), F32),
                pltpu.VMEM((4, 8, 8, 128), F32),
                pltpu.VMEM((4, 8, 8, 128), F32),
                pltpu.VMEM((4, 8, 8, 128), F32),
                pltpu.VMEM((2, 2, 8, 128), jnp.int32),
                pltpu.VMEM((2, 2, 8, 8, 128), F32),
                pltpu.VMEM((4, 128), jnp.int32),
                pltpu.VMEM((n_gx, 1, 128), F32),
                pltpu.VMEM((2, 2, 2, 4, 8, 128), F32),
                pltpu.SemaphoreType.DMA((22,)),
                pltpu.SemaphoreType.DMA((22,)),
                pltpu.SemaphoreType.DMA,
                pltpu.SemaphoreType.DMA,
                pltpu.SemaphoreType.REGULAR((2,)),
                pltpu.SemaphoreType.DMA((4,)),
            ],
            compiler_params=pltpu.CompilerParams(collective_id=0, has_side_effects=True, vmem_limit_bytes=8 * 1024 * 1024),
            name="reach",
        )(*[pltpu.with_memory_space_constraint(x, pltpu.HBM) for x in (value_field, wind_grid, obstacle)])

    placed = (P(None, "gx", "ha", None), P(None, None, "gx", None), P("gx", None))
    return jax.shard_map(
        local, mesh=mesh, in_specs=placed, out_specs=P(None, "gx", "ha", None), check_vma=False
    )
```
